32 devices in a mesh: space: 4 (over x, core), vel: 8 (over z, y).
Axes of the slice: x: 2, y: 2, z: 4, core: 2. Of those that a mesh axis runs over, the one named last changes fastest.
Arguments:
- particles: float32 [2048, 32768], P('space', 'vel'), may hold values from 0.1 to 2
- gain_spectrum: float32 [32, 32, 32], replicated, may hold values from 0 to 1
- freq_spectrum: float32 [32, 32, 32], replicated, may hold values from 0 to 1
- panel_temp: float32 [32], replicated, may hold values from 0.5 to 4
- wall_cells: int32 [32, 16], replicated, may hold values from 0 to 2047, as said below
Outputs:
- particles_out: float32 [2048, 32768], P('space', 'vel')
The draws below stay inside these ranges and needn't reach their ends.
Inputs may be any that keep to these rules, and one draw needn't show every extreme that they name: `wall_cells`: all 512 entries are distinct cells, so each wall cell belongs to one panel.
All inputs are finite; a program needn't handle non-finite values.
Results may differ from the reference program's by a relative error of at most 0.000059.
Values sent between devices are 32-bit elements; how exact they have to be, the bound alone decides.
No kernel may reach another device: no remote copies, remote signals or barrier semaphores. Data moves between devices by JAX's collectives and lax.ppermute only.
A program may use at most 256 MiB of HBM per device.

```python
import math
import jax
import jax.numpy as jnp
from jax import lax

NV1 = 32
NVEL = 32768
CELLS = 2048
PANELS = 32
CPP = 16


def draw_wall_cells(key, part):
    wall_total = PANELS * CPP
    inner_ids = jax.random.permutation(jax.random.fold_in(key, 1), CELLS - 2)[:wall_total - 2] + 1
    chosen = jnp.concatenate([jnp.array([0, CELLS - 1], dtype=jnp.int32), inner_ids.astype(jnp.int32)])
    shuffle = jax.random.permutation(jax.random.fold_in(key, 2), wall_total)
    return chosen[shuffle].reshape(PANELS, CPP).astype(jnp.int32)


def steps_of(stream_key, dims, cuts, least, high):
    def one(axis_at, parts):
        heights = jax.random.uniform(jax.random.fold_in(jax.random.fold_in(stream_key, 6), axis_at), (parts,), jnp.float32, least / len(cuts), high / len(cuts))
        return jnp.repeat(jnp.exp(heights), dims[axis_at] // parts).reshape((-1,) + (1,) * (len(dims) - axis_at - 1))

    gain = one(*cuts[0])
    for cut in cuts[1:]:
        gain = gain * one(*cut)
    return gain


def setup_inputs(seed: int = 0) -> dict:
    seeds = jax.random.split(jax.random.key(seed), 6)
    particles = jnp.clip(0.1 + 1.9 * jax.random.uniform(seeds[0], (CELLS, NVEL), jnp.float32) ** steps_of(seeds[0], (CELLS, NVEL), ((0, 4), (1, 8)), -0.2, 0.2), 0.1, 2.0)
    gain_spectrum = jnp.clip(jax.random.uniform(seeds[1], (NV1, NV1, NV1), jnp.float32, 0.0, 1.0), 0.0, 1.0)
    freq_spectrum = jnp.clip(jax.random.uniform(seeds[2], (NV1, NV1, NV1), jnp.float32, 0.0, 1.0), 0.0, 1.0)
    panel_temp = jnp.clip(jnp.exp(jax.random.uniform(seeds[3], (PANELS,), jnp.float32, math.log(0.5), math.log(4.0))), 0.5, 4.0)
    wall_cells = draw_wall_cells(jax.random.fold_in(seeds[5], 71), 0)
    return {"particles": particles, "gain_spectrum": gain_spectrum, "freq_spectrum": freq_spectrum, "panel_temp": panel_temp, "wall_cells": wall_cells}


courant = 0.9
top_speed = 3.0
collide_rate = 0.5
accommodation = 0.8


def reference(particles, gain_spectrum, freq_spectrum, panel_temp, wall_cells):
    plane_index = jnp.arange(NVEL, dtype=jnp.int32) // (NV1 * NV1)
    courant_col = courant * (2 * plane_index + 1 - NV1).astype(jnp.float32) / NV1
    padded = jnp.pad(particles, ((1, 1), (0, 0)))
    left_cells = padded[:-2]
    right_cells = padded[2:]
    moved = jnp.where(courant_col > 0, particles - courant_col * (particles - left_cells), particles - courant_col * (right_cells - particles))
    block_size = math.gcd(CELLS, 256)

    def collide(block_rows):
        cube_rows = block_rows.reshape(block_size, NV1, NV1, NV1)
        spectrum = jnp.fft.fftn(cube_rows, axes=(1, 2, 3))
        gain_part = jnp.real(jnp.fft.ifftn(spectrum * gain_spectrum, axes=(1, 2, 3)))
        freq_part = jnp.real(jnp.fft.ifftn(spectrum * freq_spectrum, axes=(1, 2, 3)))
        result = cube_rows + collide_rate * (gain_part - cube_rows * freq_part)
        return result.reshape(block_size, NVEL).astype(jnp.float32)

    post = lax.map(collide, moved.reshape(CELLS // block_size, block_size, NVEL)).reshape(CELLS, NVEL)
    velocity = top_speed * (2 * jnp.arange(NV1, dtype=jnp.int32) + 1 - NV1).astype(jnp.float32) / NV1
    speed_sq = (velocity[:, None, None] ** 2 + velocity[None, :, None] ** 2) + velocity[None, None, :] ** 2
    speed_sq = speed_sq.reshape(NVEL)
    profile = jnp.exp(-speed_sq[None, :] / (2.0 * panel_temp[:, None]))
    maxwellian = profile / jnp.sum(profile, axis=1, keepdims=True)
    wall_rows = post[wall_cells]
    wall_mass = jnp.sum(wall_rows, axis=(1, 2))
    new_rows = wall_rows + accommodation * ((wall_mass / CPP)[:, None, None] * maxwellian[:, None, :] - wall_rows)
    return post.at[wall_cells.reshape(-1)].set(new_rows.reshape(PANELS * CPP, NVEL))
```

```python
import functools
import math

import jax
import jax.numpy as jnp
import numpy as np
from jax import lax
from jax.experimental import pallas as pl
from jax.experimental.pallas import tpu as pltpu
from jax.sharding import PartitionSpec as P

courant = 0.9
top_speed = 3.0
collide_rate = 0.5
accommodation = 0.8
highest = lax.Precision.HIGHEST
sub = 8
lane = 128
parts = 2
vmem_bytes = 56 * 2**20


def split_table(table):
    high = table.astype(np.float32).astype(jnp.bfloat16)
    low = (table - high.astype(np.float64)).astype(np.float32).astype(jnp.bfloat16)
    return jnp.asarray(high), jnp.asarray(low)


def dft_tables(points):
    half = points // 2
    plane = points * points
    self_modes = [(0, 0), (0, half), (half, 0), (half, half)]
    reps = [(kb, kc) for kb in range(points) for kc in range(1, half)]
    reps += [(kb, 0) for kb in range(1, half)] + [(kb, half) for kb in range(1, half)]
    pairs = [(self_modes[0], self_modes[1]), (self_modes[2], self_modes[3])]
    slots = len(reps) + len(pairs)
    outer, inner = np.divmod(np.arange(plane), points)

    def angle(mode):
        return 2.0 * np.pi / points * ((outer * mode[0] + inner * mode[1]) % points)

    to_modes = np.zeros((plane, plane))
    from_modes = np.zeros((plane, plane))
    for slot, mode in enumerate(reps):
        theta = angle(mode)
        to_modes[:, slot] = np.cos(theta)
        to_modes[:, slots + slot] = -np.sin(theta)
        from_modes[slot] = 2.0 * np.cos(theta)
        from_modes[slots + slot] = -2.0 * np.sin(theta)
    for slot, (first, second) in enumerate(pairs, len(reps)):
        to_modes[:, slot] = from_modes[slot] = np.cos(angle(first))
        to_modes[:, slots + slot] = from_modes[slots + slot] = np.cos(angle(second))
    from_modes /= points * plane
    line = np.arange(points)
    theta = 2.0 * np.pi / points * (line[:, None] * line[None, :] % points)
    forward = np.block([[np.cos(theta), np.sin(theta)], [-np.sin(theta), np.cos(theta)]])
    forward = np.kron(forward, np.eye(sub))

    pick = np.zeros((2, plane, slots + lane), np.float32)

    def add(mode, column, weight):
        kb, kc = mode
        pick[0, kb * points + kc, column] += 0.5 * weight
        pick[1, -kb % points * points + -kc % points, column] += 0.5 * weight

    for slot, mode in enumerate(reps):
        add(mode, slot, 1.0)
    for slot, (first, second) in enumerate(pairs, len(reps)):
        add(first, slot, 0.5)
        add(second, slot, 0.5)
        add(first, slot + lane, 0.5)
        add(second, slot + lane, -0.5)
    return {
        "to_modes": split_table(to_modes),
        "from_modes": split_table(from_modes),
        "forward": split_table(forward),
        "backward": split_table(forward.T),
        "pick": jnp.asarray(pick.reshape(2 * plane, slots + lane)),
    }


def multipliers(spectrum, pick):
    points = spectrum.shape[0]
    rows = spectrum.reshape(points, points * points)
    mirrored = jnp.concatenate([rows[:1], lax.rev(rows[1:], (0,))], axis=0)
    both = jnp.concatenate([rows, mirrored], axis=1)
    return jnp.repeat(jnp.dot(both, pick, precision=highest), sub, axis=0)


def split(values):
    high = values.astype(jnp.bfloat16)
    return high, (values - high.astype(jnp.float32)).astype(jnp.bfloat16)


def dot(a, b):
    return jnp.dot(a, b, preferred_element_type=jnp.float32)


def move_kernel(rows_total, first_block, turn, body, before, after, low, high, nu, out):
    step = pl.program_id(0)
    block = jnp.where(step < turn[0], first_block + step, turn[1] + step)
    rows = body.shape[0]
    here = body[...]
    row = lax.broadcasted_iota(jnp.int32, here.shape, 0)
    first = jnp.where(block == 0, low[...], before[sub - 1 :, :])
    last = jnp.where(block == rows_total // rows - 1, high[...], after[:1, :])
    left = jnp.where(row == 0, first, pltpu.roll(here, 1, 0))
    right = jnp.where(row == rows - 1, last, pltpu.roll(here, rows - 1, 0))
    drift = nu[...]
    rising = jnp.broadcast_to(drift > 0, here.shape)
    out[...] = here - drift * jnp.where(rising, here - left, right - here)


def move(particles, low, high, nu, first_block, turn, count, rows):
    total, width = particles.shape
    per = rows // sub

    def block(step):
        return jnp.where(step < turn[0], first_block + step, turn[1] + step)

    return pl.pallas_call(
        functools.partial(move_kernel, total, first_block, turn),
        grid=(count,),
        in_specs=[
            pl.BlockSpec((rows, width), lambda i: (block(i), 0)),
            pl.BlockSpec((sub, width), lambda i: (jnp.maximum(block(i) * per - 1, 0), 0)),
            pl.BlockSpec((sub, width), lambda i: (jnp.minimum((block(i) + 1) * per, total // sub - 1), 0)),
            pl.BlockSpec((1, width), lambda i: (0, 0)),
            pl.BlockSpec((1, width), lambda i: (0, 0)),
            pl.BlockSpec((1, width), lambda i: (0, 0)),
        ],
        out_specs=pl.BlockSpec((rows, width), lambda i: (i, 0)),
        out_shape=jax.ShapeDtypeStruct((count * rows, width), jnp.float32),
        compiler_params=pltpu.CompilerParams(vmem_limit_bytes=vmem_bytes),
        cost_estimate=pl.CostEstimate(
            flops=5 * count * rows * width, bytes_accessed=8 * count * rows * width, transcendentals=0
        ),
    )(particles, particles, particles, low, high, nu)


def collide_kernel(
    x, to_high, to_low, from_high, from_low, ahead_high, ahead_low, back_high, back_low, gain, freq,
    out, mass, wide_high, wide_low, mid, both_high, both_low, fields,
):
    sources, cells, width = x.shape
    plane = to_high.shape[0]
    slots = plane // 2
    planes = width // plane
    points = sources * planes
    groups = cells // sub
    chunk = points * sub
    tile = min(256, plane)

    def where_of(a):
        return a // planes, slice(a % planes * plane, (a % planes + 1) * plane)

    for group in range(groups):
        for a in range(points):
            source, columns = where_of(a)
            mid[(group * points + a) * sub : (group * points + a + 1) * sub, :] = x[
                source, group * sub : (group + 1) * sub, columns
            ]
    high, low = split(mid[...])
    wide_high[: groups * chunk, :] = high
    wide_low[: groups * chunk, :] = low

    @pl.loop(0, plane // tile)
    def _(at):
        columns = pl.ds(pl.multiple_of(at * tile, tile), tile)
        table = to_high[:, columns]
        mid[:, columns] = (
            dot(wide_low[: groups * chunk, :], table)
            + dot(wide_high[: groups * chunk, :], to_low[:, columns])
            + dot(wide_high[: groups * chunk, :], table)
        )

    @pl.loop(0, groups)
    def _(group):
        rows = pl.ds(pl.multiple_of(group * chunk, chunk), chunk)
        spectrum = jnp.concatenate([mid[rows, :slots], mid[rows, slots:]], axis=0)
        high, low = split(spectrum)
        waves = dot(ahead_high[...], low) + dot(ahead_low[...], high) + dot(ahead_high[...], high)
        real, imag = waves[:chunk], waves[chunk:]

        def mirror(values):
            tail = values[:, slots - lane :]
            turned = [tail[-a % points * sub : (-a % points + 1) * sub] for a in range(points)]
            return jnp.concatenate(turned, axis=0)

        real_tail, imag_tail = mirror(real), mirror(imag)
        for index, table in enumerate((gain, freq)):
            pad = jnp.zeros((chunk, slots - lane), jnp.float32)
            extra = table[:, slots:]
            upper = real * table[:, :slots] + jnp.concatenate([pad, real_tail * extra], axis=1)
            lower = imag * table[:, :slots] - jnp.concatenate([pad, imag_tail * extra], axis=1)
            for start, values in ((0, upper), (chunk, lower)):
                high, low = split(values)
                both_high[start : start + chunk, index * slots : (index + 1) * slots] = high
                both_low[start : start + chunk, index * slots : (index + 1) * slots] = low
        for index in range(2):
            columns = slice(index * slots, (index + 1) * slots)
            lines = (
                dot(back_high[...], both_low[:, columns])
                + dot(back_low[...], both_high[:, columns])
                + dot(back_high[...], both_high[:, columns])
            )
            high, low = split(jnp.concatenate([lines[:chunk], lines[chunk:]], axis=1))
            at = pl.ds(pl.multiple_of((index * groups + group) * chunk, chunk), chunk)
            wide_high[at, :] = high
            wide_low[at, :] = low

    @pl.loop(0, plane // tile)
    def _(at):
        columns = pl.ds(pl.multiple_of(at * tile, tile), tile)
        table = from_high[:, columns]
        fields[:, columns] = (
            dot(wide_low[...], table) + dot(wide_high[...], from_low[:, columns]) + dot(wide_high[...], table)
        )

    for group in range(groups):
        total = jnp.zeros((sub, plane), jnp.float32)
        for a in range(points):
            source, columns = where_of(a)
            start = (group * points + a) * sub
            cells_here = slice(group * sub, (group + 1) * sub)
            here = x[source, cells_here, columns]
            gained = fields[start : start + sub, :]
            lost = fields[groups * chunk + start : groups * chunk + start + sub, :]
            post = here + collide_rate * (gained - here * lost)
            out[source, cells_here, columns] = post
            total = total + post
        lanes = total[:, :lane]
        for at in range(lane, plane, lane):
            lanes = lanes + total[:, at : at + lane]
        mass[group * sub : (group + 1) * sub, :] = lanes


def collide(cubes, tables, gain, freq):
    sources, cells, width = cubes.shape
    plane = tables["to_modes"][0].shape[0]
    points = sources * width // plane
    step = math.gcd(cells, 2 * sub)
    chunk = step * points
    operands = [*tables["to_modes"], *tables["from_modes"], *tables["forward"], *tables["backward"], gain, freq]
    whole = pl.BlockSpec(memory_space=pltpu.VMEM)
    bf16, f32 = jnp.bfloat16, jnp.float32
    multiply_adds = 3 * cells * points * (3 * plane * plane + 6 * points * sub * plane)
    return pl.pallas_call(
        collide_kernel,
        grid=(cells // step,),
        in_specs=[pl.BlockSpec((sources, step, width), lambda i: (0, i, 0))] + [whole] * len(operands),
        out_specs=[
            pl.BlockSpec((sources, step, width), lambda i: (0, i, 0)),
            pl.BlockSpec((step, lane), lambda i: (i, 0)),
        ],
        out_shape=[
            jax.ShapeDtypeStruct(cubes.shape, f32),
            jax.ShapeDtypeStruct((cells, lane), f32),
        ],
        scratch_shapes=[
            pltpu.VMEM((2 * chunk, plane), bf16),
            pltpu.VMEM((2 * chunk, plane), bf16),
            pltpu.VMEM((chunk, plane), f32),
            pltpu.VMEM((2 * points * sub, plane), bf16),
            pltpu.VMEM((2 * points * sub, plane), bf16),
            pltpu.VMEM((2 * chunk, plane), f32),
        ],
        compiler_params=pltpu.CompilerParams(vmem_limit_bytes=vmem_bytes),
        cost_estimate=pl.CostEstimate(
            flops=2 * multiply_adds, bytes_accessed=8 * cubes.size, transcendentals=0
        ),
    )(cubes, *operands)


def settle_kernel(post, member, emit_high, emit_low, *rest):
    out = rest[-1]
    chosen = member[...]
    share = jnp.sum(chosen, axis=1, keepdims=True)
    picked = chosen.astype(jnp.bfloat16)
    emission = dot(picked, emit_low[...]) + dot(picked, emit_high[...])
    out[...] = post[...] + accommodation * (emission - share * post[...])


def settle(post, member, emit, earlier, shape, first_block, turn, rows):
    count = post.shape[0] // rows
    width = post.shape[1]
    panels = member.shape[1]

    def block(step):
        return jnp.where(step < turn[0], first_block + step, turn[1] + step)

    operands = [post, member, *emit]
    in_specs = [
        pl.BlockSpec((rows, width), lambda i: (i, 0)),
        pl.BlockSpec((rows, panels), lambda i: (i, 0)),
        pl.BlockSpec((panels, width), lambda i: (0, 0)),
        pl.BlockSpec((panels, width), lambda i: (0, 0)),
    ]
    aliases = {}
    if earlier is not None:
        aliases = {len(operands): 0}
        operands.append(earlier)
        in_specs.append(pl.BlockSpec(memory_space=pl.ANY))
    return pl.pallas_call(
        settle_kernel,
        grid=(count,),
        in_specs=in_specs,
        out_specs=pl.BlockSpec((rows, width), lambda i: (block(i), 0)),
        out_shape=jax.ShapeDtypeStruct(shape, jnp.float32),
        input_output_aliases=aliases,
        compiler_params=pltpu.CompilerParams(vmem_limit_bytes=vmem_bytes),
        cost_estimate=pl.CostEstimate(
            flops=4 * panels * post.size, bytes_accessed=8 * post.size, transcendentals=0
        ),
    )(*operands)


def on_device(particles, gain_spectrum, freq_spectrum, panel_temp, wall_cells):
    cell_dev, vel_dev = particles.shape
    points = gain_spectrum.shape[0]
    plane_size = points * points
    planes = vel_dev // plane_size
    vel_count = lax.axis_size("vel")
    vel_at = lax.axis_index("vel")
    space_at = lax.axis_index("space")
    space_count = lax.axis_size("space")
    tables = dft_tables(points)

    columns = jnp.arange(vel_dev, dtype=jnp.int32)
    plane_index = vel_at * planes + columns // plane_size
    nu = (courant * (2 * plane_index + 1 - points).astype(jnp.float32) / points)[None, :]

    up = [(i, i + 1) for i in range(space_count - 1)]
    down = [(i + 1, i) for i in range(space_count - 1)]
    low = lax.ppermute(particles[-1:], "space", up)
    high = lax.ppermute(particles[:1], "space", down)

    rows = math.gcd(cell_dev // (2 * parts), 32)
    blocks = cell_dev // rows
    quarter, half = blocks // 4, blocks // 2
    zero = jnp.zeros((1, vel_dev), jnp.float32)
    plans = [(quarter, (half, 0)), (0, (quarter, half))]
    edges = [(zero, zero), (low, high)]
    share = half * rows // vel_count

    def cells_of(plan):
        first_block, turn = plan
        step = jnp.arange(half, dtype=jnp.int32)
        block = jnp.where(step < turn[0], first_block + step, turn[1] + step)
        at = block[:, None] * rows + jnp.arange(rows, dtype=jnp.int32)[None, :]
        return space_at * cell_dev + at.reshape(-1)

    def membership(cell_ids):
        panels, per_panel = wall_cells.shape
        hit = wall_cells.reshape(1, panels, per_panel) == cell_ids[:, None, None]
        return jnp.any(hit, axis=2).astype(jnp.float32)

    arrived = []
    for plan, edge in zip(plans, edges):
        moved = move(particles, *edge, nu, *plan, half, rows)
        moved = moved.reshape(vel_count, share, vel_dev)
        arrived.append(lax.all_to_all(moved, "vel", 0, 0, tiled=True))

    gain = multipliers(gain_spectrum, tables["pick"])
    freq = multipliers(freq_spectrum, tables["pick"])
    panels, per_panel = wall_cells.shape
    members = [membership(cells_of(plan)) for plan in plans]
    returned = []
    part_mass = jnp.zeros((panels,), jnp.float32)
    for cubes, member in zip(arrived, members):
        post, mass = collide(cubes, tables, gain, freq)
        returned.append(lax.all_to_all(post, "vel", 0, 0, tiled=True))
        mine = lax.dynamic_slice_in_dim(member, vel_at * share, share, axis=0)
        part_mass = part_mass + jnp.sum(mine * jnp.sum(mass, axis=1)[:, None], axis=0)
    wall_mass = lax.psum(part_mass, ("space", "vel"))

    line = jnp.arange(points, dtype=jnp.int32)
    velocity = top_speed * (2 * line + 1 - points).astype(jnp.float32) / points
    line_weight = jnp.exp(-(velocity**2)[None, :] / (2.0 * panel_temp[:, None]))
    normal_sum = jnp.sum(line_weight, axis=1) ** 3

    def speed(index):
        return top_speed * (2 * index + 1 - points).astype(jnp.float32) / points

    speed_sq = speed(plane_index) ** 2 + speed(columns // points % points) ** 2 + speed(columns % points) ** 2
    profile = jnp.exp(-speed_sq[None, :] / (2.0 * panel_temp[:, None]))
    maxwellian = profile / normal_sum[:, None]
    emission = (wall_mass / per_panel)[:, None] * maxwellian
    emit_high = lax.reduce_precision(emission, exponent_bits=8, mantissa_bits=7)
    emit = (emit_high.astype(jnp.bfloat16), (emission - emit_high).astype(jnp.bfloat16))

    out = None
    for back, member, plan in zip(returned, members, plans):
        out = settle(back.reshape(half * rows, vel_dev), member, emit, out, particles.shape, *plan, rows)
    return out


def solution(mesh):
    in_specs = (P("space", "vel"), P(), P(), P(), P())
    out_specs = P("space", "vel")
    return jax.shard_map(on_device, mesh=mesh, in_specs=in_specs, out_specs=out_specs, check_vma=False)
```

```python
import functools
import math

import jax
import jax.numpy as jnp
import numpy as np
from jax import lax
from jax.experimental import pallas as pl
from jax.experimental.pallas import tpu as pltpu
from jax.sharding import PartitionSpec as P

courant = 0.9
top_speed = 3.0
collide_rate = 0.5
accommodation = 0.8
highest = lax.Precision.HIGHEST
sub = 8
lane = 128
vmem_bytes = 56 * 2**20


def split_table(table):
    high = table.astype(np.float32).astype(jnp.bfloat16)
    low = (table - high.astype(np.float64)).astype(np.float32).astype(jnp.bfloat16)
    return jnp.asarray(high), jnp.asarray(low)


def dft_tables(points):
    half = points // 2
    plane = points * points
    self_modes = [(0, 0), (0, half), (half, 0), (half, half)]
    reps = [(kb, kc) for kb in range(points) for kc in range(1, half)]
    reps += [(kb, 0) for kb in range(1, half)] + [(kb, half) for kb in range(1, half)]
    pairs = [(self_modes[0], self_modes[1]), (self_modes[2], self_modes[3])]
    slots = len(reps) + len(pairs)
    outer, inner = np.divmod(np.arange(plane), points)

    def angle(mode):
        return 2.0 * np.pi / points * ((outer * mode[0] + inner * mode[1]) % points)

    to_modes = np.zeros((plane, plane))
    from_modes = np.zeros((plane, plane))
    for slot, mode in enumerate(reps):
        theta = angle(mode)
        to_modes[:, slot] = np.cos(theta)
        to_modes[:, slots + slot] = -np.sin(theta)
        from_modes[slot] = 2.0 * np.cos(theta)
        from_modes[slots + slot] = -2.0 * np.sin(theta)
    for slot, (first, second) in enumerate(pairs, len(reps)):
        to_modes[:, slot] = from_modes[slot] = np.cos(angle(first))
        to_modes[:, slots + slot] = from_modes[slots + slot] = np.cos(angle(second))
    from_modes /= points * plane
    line = np.arange(points)
    theta = 2.0 * np.pi / points * (line[:, None] * line[None, :] % points)
    forward = np.block([[np.cos(theta), np.sin(theta)], [-np.sin(theta), np.cos(theta)]])
    forward = np.kron(forward, np.eye(sub))

    pick = np.zeros((2, plane, slots + lane), np.float32)

    def add(mode, column, weight):
        kb, kc = mode
        pick[0, kb * points + kc, column] += 0.5 * weight
        pick[1, -kb % points * points + -kc % points, column] += 0.5 * weight

    for slot, mode in enumerate(reps):
        add(mode, slot, 1.0)
    for slot, (first, second) in enumerate(pairs, len(reps)):
        add(first, slot, 0.5)
        add(second, slot, 0.5)
        add(first, slot + lane, 0.5)
        add(second, slot + lane, -0.5)
    return {
        "to_modes": split_table(to_modes),
        "from_modes": split_table(from_modes),
        "forward": split_table(forward),
        "backward": split_table(forward.T),
        "pick": jnp.asarray(pick.astype(jnp.bfloat16)),
    }


def split(values):
    high = values.astype(jnp.bfloat16)
    return high, (values - high.astype(jnp.float32)).astype(jnp.bfloat16)


def dot(a, b):
    return jnp.dot(a, b, preferred_element_type=jnp.float32)


def multiplier_kernel(gain, freq, pick, gain_out, freq_out):
    points = gain.shape[0]
    rows = jnp.concatenate([gain[...], freq[...]], axis=0)
    high, _ = split(rows)
    mid, low = split(rows - high.astype(jnp.float32))
    here, mirrored = (dot(low, pick[i]) + dot(mid, pick[i]) + dot(high, pick[i]) for i in range(2))
    for index, out in enumerate((gain_out, freq_out)):
        for a in range(points):
            at, turned = index * points + a, index * points + -a % points
            row = here[at : at + 1] + mirrored[turned : turned + 1]
            out[a * sub : (a + 1) * sub, :] = jnp.broadcast_to(row, (sub, row.shape[1]))


def multipliers(gain_spectrum, freq_spectrum, pick):
    points = gain_spectrum.shape[0]
    out = jax.ShapeDtypeStruct((points * sub, pick.shape[2]), jnp.float32)
    return pl.pallas_call(
        multiplier_kernel,
        in_specs=[local(pltpu.VMEM)] * 3,
        out_specs=[local(pltpu.VMEM)] * 2,
        out_shape=[out, out],
        compiler_params=pltpu.CompilerParams(vmem_limit_bytes=vmem_bytes),
        cost_estimate=pl.CostEstimate(flops=24 * points * pick.size, bytes_accessed=2 * pick.size, transcendentals=0),
    )(gain_spectrum.reshape(points, -1), freq_spectrum.reshape(points, -1), pick)


def partners(count):
    far = tuple(range(count // 2, count))
    return far, tuple(sorted(range(1, count // 2), key=lambda step: (-step.bit_length(), step)))


def swap(values, axis, step):
    return lax.ppermute(values, axis, [(i, i ^ step) for i in range(lax.axis_size(axis))])


def local(array):
    return pl.BlockSpec(memory_space=array)


def start_of(group, cells, low_groups, gap):
    return pl.multiple_of(group * cells + jnp.where(group < low_groups, 0, gap), sub)


def move_kernel(order, offset, low_groups, gap, points, has_halo, has_after, has_edges, me, particles, *rest):
    count = len(order)
    low, high = rest[:2] if has_halo else (None, None)
    outs = rest[2 * has_halo + has_after :][:count]
    edges = rest[2 * has_halo + has_after + count :][: 2 * has_edges]
    inside, made, rim, in_sems, out_sems = rest[-5:]
    cells, width = outs[0].shape
    total = particles.shape[0]
    planes = width // points**2
    span = inside.shape[1]
    at = me[0]

    def place(step):
        first = offset + start_of(at ^ step, cells, low_groups, gap)
        begin = pl.multiple_of(jnp.clip(first - sub, 0, total - span), sub)
        return first, begin

    def fetch(k, step):
        return pltpu.make_async_copy(particles.at[pl.ds(place(step)[1], span)], inside.at[k], in_sems.at[k])

    def store(k):
        return pltpu.make_async_copy(made.at[k], outs[k], out_sems.at[k])

    def edge_in(k):
        rows = pl.ds((total - sub) * k, sub)
        return pltpu.make_async_copy(particles.at[rows], rim.at[k], in_sems.at[count + k])

    def edge_out(k):
        return pltpu.make_async_copy(rim.at[k], edges[k], out_sems.at[count + k])

    for k, step in enumerate(order):
        fetch(k, step).start()
    for k in range(len(edges)):
        edge_in(k).start()
    for k, step in enumerate(order):
        fetch(k, step).wait()
        first, begin = place(step)
        skip = pl.multiple_of(first - begin, sub)
        ahead = pl.multiple_of(jnp.maximum(skip - sub, 0), sub)
        behind = pl.multiple_of(jnp.minimum(skip + cells, span - sub), sub)
        for plane in range(planes):
            columns = slice(plane * points**2, (plane + 1) * points**2)
            nu = courant * (2 * (at * planes + plane) + 1 - points).astype(jnp.float32) / points
            here = inside[k, pl.ds(skip, cells), columns]
            before = inside[k, pl.ds(ahead, sub), columns][sub - 1 :, :]
            after = inside[k, pl.ds(behind, sub), columns][:1, :]
            if has_halo:
                before = jnp.where(first == 0, low[sub - 1 :, columns], before)
                after = jnp.where(first + cells == total, high[:1, columns], after)
            row = lax.broadcasted_iota(jnp.int32, here.shape, 0)
            left = jnp.where(row == 0, before, pltpu.roll(here, 1, 0))
            right = jnp.where(row == cells - 1, after, pltpu.roll(here, cells - 1, 0))
            made[k, :, columns] = here - nu * jnp.where(nu > 0, here - left, right - here)
        store(k).start()
    for k in range(len(edges)):
        edge_in(k).wait()
        edge_out(k).start()
    for k in range(len(edges)):
        edge_out(k).wait()
    for k in range(count):
        store(k).wait()


def move(me, particles, order, cells, offset, low_groups, gap, points, halo=(), after=(), edges=False):
    total, width = particles.shape
    count = len(order)
    span = min(cells + 2 * sub, total)
    size = count * cells * width
    shape = jax.ShapeDtypeStruct((cells, width), jnp.float32)
    rim = jax.ShapeDtypeStruct((sub, width), jnp.float32)
    flags = (bool(halo), len(after), edges)
    return pl.pallas_call(
        functools.partial(move_kernel, order, offset, low_groups, gap, points, *flags),
        in_specs=[local(pltpu.SMEM), local(pltpu.HBM)]
        + [local(pltpu.VMEM)] * len(halo)
        + [local(pltpu.HBM)] * len(after),
        out_specs=[local(pltpu.HBM)] * (count + 2 * edges),
        out_shape=[shape] * count + [rim] * (2 * edges),
        scratch_shapes=[
            pltpu.VMEM((count, span, width), jnp.float32),
            pltpu.VMEM((count, cells, width), jnp.float32),
            pltpu.VMEM((2, sub, width), jnp.float32),
            pltpu.SemaphoreType.DMA((count + 2,)),
            pltpu.SemaphoreType.DMA((count + 2,)),
        ],
        compiler_params=pltpu.CompilerParams(vmem_limit_bytes=vmem_bytes),
        cost_estimate=pl.CostEstimate(flops=5 * size, bytes_accessed=10 * size, transcendentals=0),
    )(me, particles, *halo, *after)


def collide_kernel(steps, me, *rest):
    count = len(steps)
    xs, rest = rest[:count], rest[count:]
    to_high, to_low, from_high, from_low, ahead_high, ahead_low, back_high, back_low, gain, freq = rest[:10]
    outs, rest = rest[10 : 10 + count], rest[10 + count :]
    mass, wide_high, wide_low, mid, both_high, both_low, fields = rest
    cells, width = xs[0].shape
    plane = to_high.shape[0]
    slots = plane // 2
    planes = width // plane
    points = count * planes
    groups = cells // sub
    chunk = points * sub
    tile = min(256, plane)
    at = me[0]

    def pieces():
        for k, step in enumerate(steps):
            for group in range(groups):
                for j in range(planes):
                    start = (group * points + (at ^ step) * planes + j) * sub
                    here = (slice(group * sub, (group + 1) * sub), slice(j * plane, (j + 1) * plane))
                    yield k, group, here, pl.multiple_of(start, sub)

    for k, group, here, start in pieces():
        mid[pl.ds(start, sub), :] = xs[k][here]
    high, low = split(mid[...])
    wide_high[: groups * chunk, :] = high
    wide_low[: groups * chunk, :] = low

    @pl.loop(0, plane // tile)
    def _(at):
        columns = pl.ds(pl.multiple_of(at * tile, tile), tile)
        table = to_high[:, columns]
        mid[:, columns] = (
            dot(wide_low[: groups * chunk, :], table)
            + dot(wide_high[: groups * chunk, :], to_low[:, columns])
            + dot(wide_high[: groups * chunk, :], table)
        )

    @pl.loop(0, groups)
    def _(group):
        rows = pl.ds(pl.multiple_of(group * chunk, chunk), chunk)
        spectrum = jnp.concatenate([mid[rows, :slots], mid[rows, slots:]], axis=0)
        high, low = split(spectrum)
        waves = dot(ahead_high[...], low) + dot(ahead_low[...], high) + dot(ahead_high[...], high)
        real, imag = waves[:chunk], waves[chunk:]

        def mirror(values):
            tail = values[:, slots - lane :]
            turned = [tail[-a % points * sub : (-a % points + 1) * sub] for a in range(points)]
            return jnp.concatenate(turned, axis=0)

        real_tail, imag_tail = mirror(real), mirror(imag)
        for index, table in enumerate((gain, freq)):
            pad = jnp.zeros((chunk, slots - lane), jnp.float32)
            extra = table[:, slots:]
            upper = real * table[:, :slots] + jnp.concatenate([pad, real_tail * extra], axis=1)
            lower = imag * table[:, :slots] - jnp.concatenate([pad, imag_tail * extra], axis=1)
            for start, values in ((0, upper), (chunk, lower)):
                high, low = split(values)
                both_high[start : start + chunk, index * slots : (index + 1) * slots] = high
                both_low[start : start + chunk, index * slots : (index + 1) * slots] = low
        for index in range(2):
            columns = slice(index * slots, (index + 1) * slots)
            lines = (
                dot(back_high[...], both_low[:, columns])
                + dot(back_low[...], both_high[:, columns])
                + dot(back_high[...], both_high[:, columns])
            )
            high, low = split(jnp.concatenate([lines[:chunk], lines[chunk:]], axis=1))
            at = pl.ds(pl.multiple_of((index * groups + group) * chunk, chunk), chunk)
            wide_high[at, :] = high
            wide_low[at, :] = low

    @pl.loop(0, plane // tile)
    def _(at):
        columns = pl.ds(pl.multiple_of(at * tile, tile), tile)
        table = from_high[:, columns]
        fields[:, columns] = (
            dot(wide_low[...], table) + dot(wide_high[...], from_low[:, columns]) + dot(wide_high[...], table)
        )

    totals = [jnp.zeros((sub, plane), jnp.float32)] * groups
    for k, group, here, start in pieces():
        cube = xs[k][here]
        gained = fields[pl.ds(start, sub), :]
        lost = fields[pl.ds(pl.multiple_of(groups * chunk + start, sub), sub), :]
        post = cube + collide_rate * (gained - cube * lost)
        outs[k][here] = post
        totals[group] = totals[group] + post
    for group, total in enumerate(totals):
        lanes = total[:, :lane]
        for column in range(lane, plane, lane):
            lanes = lanes + total[:, column : column + lane]
        mass[group * sub : (group + 1) * sub, :] = lanes


def collide(me, cubes, steps, tables, gain, freq):
    cells, width = cubes[0].shape
    count = len(cubes)
    plane = tables["to_modes"][0].shape[0]
    points = count * width // plane
    step = math.gcd(cells, 2 * sub)
    chunk = step * points
    operands = [*tables["to_modes"], *tables["from_modes"], *tables["forward"], *tables["backward"], gain, freq]
    bf16, f32 = jnp.bfloat16, jnp.float32
    block = pl.BlockSpec((step, width), lambda i: (i, 0))
    multiply_adds = 3 * cells * points * (3 * plane * plane + 6 * points * sub * plane)
    *posts, mass = pl.pallas_call(
        functools.partial(collide_kernel, steps),
        grid=(cells // step,),
        in_specs=[local(pltpu.SMEM)] + [block] * count + [local(pltpu.VMEM)] * len(operands),
        out_specs=[block] * count + [pl.BlockSpec((step, lane), lambda i: (i, 0))],
        out_shape=[jax.ShapeDtypeStruct((cells, width), f32)] * count + [jax.ShapeDtypeStruct((cells, lane), f32)],
        scratch_shapes=[
            pltpu.VMEM((2 * chunk, plane), bf16),
            pltpu.VMEM((2 * chunk, plane), bf16),
            pltpu.VMEM((chunk, plane), f32),
            pltpu.VMEM((2 * points * sub, plane), bf16),
            pltpu.VMEM((2 * points * sub, plane), bf16),
            pltpu.VMEM((2 * chunk, plane), f32),
        ],
        compiler_params=pltpu.CompilerParams(vmem_limit_bytes=vmem_bytes),
        cost_estimate=pl.CostEstimate(
            flops=3 * multiply_adds, bytes_accessed=8 * count * cells * width, transcendentals=0
        ),
    )(me, *cubes, *operands)
    return posts, mass


def mass_kernel(count, *refs):
    parts, out = refs[:count], refs[-1]
    total = jnp.zeros(out.shape, jnp.float32)
    for mass, member in zip(parts[::2], parts[1::2]):
        cell = jnp.sum(mass[...], axis=1, keepdims=True)
        total = total + jnp.sum(member[...] * cell, axis=0, keepdims=True)
    out[...] = total


def panel_mass(pairs, after):
    flat = [array for pair in pairs for array in pair]
    return pl.pallas_call(
        functools.partial(mass_kernel, len(flat)),
        in_specs=[local(pltpu.VMEM)] * len(flat) + [local(pl.ANY)] * len(after),
        out_specs=local(pltpu.VMEM),
        out_shape=jax.ShapeDtypeStruct((1, flat[1].shape[1]), jnp.float32),
    )(*flat, *after)


def settle_kernel(steps, offset, low_groups, gap, me, member, emit, *rest):
    count = len(steps)
    posts = rest[:count]
    out, held, emission, in_sems, out_sems = rest[-5:]
    cells, width = held.shape[1:]
    at = me[0]

    def fetch(k):
        return pltpu.make_async_copy(posts[k], held.at[k], in_sems.at[k])

    def store(k):
        first = offset + start_of(at ^ steps[k], cells, low_groups, gap)
        return pltpu.make_async_copy(held.at[k], out.at[pl.ds(first, cells)], out_sems.at[k])

    for k in range(count):
        fetch(k).start()
    chosen = member[...]
    share = accommodation * jnp.sum(chosen, axis=1, keepdims=True)
    emission[...] = dot(jnp.concatenate([chosen, chosen], axis=1).astype(jnp.bfloat16), emit[...])
    for k in range(count):
        fetch(k).wait()
        rows = pl.ds(pl.multiple_of(k * cells, sub), cells)
        post = held[k]
        held[k] = post + (accommodation * emission[rows, :] - share[k * cells : (k + 1) * cells] * post)
        store(k).start()
    for k in range(count):
        store(k).wait()


def settle(me, posts, steps, member, emit, earlier, shape, offset, low_groups, gap):
    cells, width = posts[0].shape
    count = len(posts)
    size = count * cells * width
    operands = [me, member, emit, *posts]
    in_specs = [local(pltpu.SMEM), local(pltpu.VMEM), local(pltpu.VMEM)] + [local(pl.ANY)] * count
    aliases = {}
    if earlier is not None:
        aliases = {len(operands): 0}
        operands.append(earlier)
        in_specs.append(local(pltpu.HBM))
    return pl.pallas_call(
        functools.partial(settle_kernel, steps, offset, low_groups, gap),
        in_specs=in_specs,
        out_specs=local(pltpu.HBM),
        out_shape=jax.ShapeDtypeStruct(shape, jnp.float32),
        scratch_shapes=[
            pltpu.VMEM((count, cells, width), jnp.float32),
            pltpu.VMEM((count * cells, width), jnp.float32),
            pltpu.SemaphoreType.DMA((count,)),
            pltpu.SemaphoreType.DMA((count,)),
        ],
        input_output_aliases=aliases,
        compiler_params=pltpu.CompilerParams(vmem_limit_bytes=vmem_bytes),
        cost_estimate=pl.CostEstimate(
            flops=4 * member.shape[1] * size, bytes_accessed=8 * size, transcendentals=0
        ),
    )(*operands)


def on_device(particles, gain_spectrum, freq_spectrum, panel_temp, wall_cells):
    cell_dev, vel_dev = particles.shape
    points = gain_spectrum.shape[0]
    plane_size = points * points
    planes = vel_dev // plane_size
    vel_count = lax.axis_size("vel")
    vel_at = lax.axis_index("vel")
    space_at = lax.axis_index("space")
    space_count = lax.axis_size("space")
    me = vel_at.astype(jnp.int32)[None]
    tables = dft_tables(points)
    panels, per_panel = wall_cells.shape

    quarter, half = cell_dev // 4, cell_dev // 2
    cells = half // vel_count
    inner, outer = (quarter, vel_count, 0), (0, vel_count // 2, half)
    far, near = partners(vel_count)
    steps = (*far, *near, 0)
    urgent, ready = far[:2], (*far[:2], *near[:1], *far[2:3])

    def send(arrays):
        return {step: swap(array, "vel", step) if step else array for step, array in arrays.items()}

    def rest(done):
        return tuple(step for step in steps if step not in done)

    early = move(me, particles, urgent, cells, *inner, points)
    *late, first_rows, last_rows = move(
        me, particles, rest(urgent), cells, *inner, points, after=early[:1], edges=True
    )
    inner_cubes = send(dict(zip((*urgent, *rest(urgent)), (*early, *late))))
    space_pairs = [(i, i + 1) for i in range(space_count - 1)]
    low = lax.ppermute(last_rows, "space", space_pairs)
    high = lax.ppermute(first_rows, "space", [(target, source) for source, target in space_pairs])
    outer_early = move(me, particles, ready, cells, *outer, points, halo=(low, high))
    gain, freq = multipliers(gain_spectrum, freq_spectrum, tables["pick"])

    def collided(cubes):
        posts, mass = collide(me, [cubes[step] for step in steps], steps, tables, gain, freq)
        return dict(zip(steps, posts)), mass

    inner_posts, inner_mass = collided(inner_cubes)
    outer_late = move(
        me, particles, rest(ready), cells, *outer, points, halo=(low, high), after=(inner_mass,)
    )
    outer_cubes = send(dict(zip((*ready, *rest(ready)), (*outer_early, *outer_late))))
    outer_posts, outer_mass = collided(outer_cubes)

    def cells_of(plan, group):
        offset, low_groups, gap = plan
        first = offset + group * cells + jnp.where(group < low_groups, 0, gap)
        return space_at * cell_dev + first + jnp.arange(cells, dtype=jnp.int32)

    def membership(cell_ids):
        hit = wall_cells.reshape(1, panels, per_panel) == cell_ids[:, None, None]
        return jnp.any(hit, axis=2).astype(jnp.float32)

    held = near
    *tied, outer_mass = lax.optimization_barrier((*(inner_posts[step] for step in held), outer_mass))
    inner_back = send({**inner_posts, **dict(zip(held, tied))})
    outer_back = send(outer_posts)
    pairs = [
        (mass, membership(cells_of(plan, vel_at))) for mass, plan in ((inner_mass, inner), (outer_mass, outer))
    ]
    wall_mass = lax.psum(panel_mass(pairs, [inner_back[step] for step in (*far, *near)]), "space")
    step = 1
    while step < vel_count:
        wall_mass = wall_mass + swap(wall_mass, "vel", step)
        step *= 2

    def speed(index):
        return top_speed * (2 * index + 1 - points).astype(jnp.float32) / points

    line = jnp.arange(points, dtype=jnp.int32)
    line_weight = jnp.exp(-(speed(line) ** 2)[None, :] / (2.0 * panel_temp[:, None]))
    normal_sum = jnp.sum(line_weight, axis=1) ** 3
    columns = jnp.arange(vel_dev, dtype=jnp.int32)
    plane_index = vel_at * planes + columns // plane_size
    speed_sq = speed(plane_index) ** 2 + speed(columns // points % points) ** 2 + speed(columns % points) ** 2
    profile = jnp.exp(-speed_sq[None, :] / (2.0 * panel_temp[:, None]))
    maxwellian = profile / normal_sum[:, None]
    emission = (wall_mass.reshape(panels, 1) / per_panel) * maxwellian
    emit_high = lax.reduce_precision(emission, exponent_bits=8, mantissa_bits=7)
    emit = jnp.concatenate([emit_high, emission - emit_high], axis=0).astype(jnp.bfloat16)

    def wall(posts, part, plan, earlier):
        ids = jnp.concatenate([cells_of(plan, vel_at ^ step) for step in part])
        posts = [posts[step] for step in part]
        return settle(me, posts, part, membership(ids), emit, earlier, particles.shape, *plan)

    last = far[-2:]
    out = wall(inner_back, steps, inner, None)
    out = wall(outer_back, rest(last), outer, out)
    return wall(outer_back, last, outer, out)


def solution(mesh):
    in_specs = (P("space", "vel"), P(), P(), P(), P())
    out_specs = P("space", "vel")
    return jax.shard_map(on_device, mesh=mesh, in_specs=in_specs, out_specs=out_specs, check_vma=False)
```

```python
import functools
import math

import jax
import jax.numpy as jnp
import numpy as np
from jax import lax
from jax.experimental import pallas as pl
from jax.experimental.pallas import tpu as pltpu
from jax.sharding import PartitionSpec as P

courant = 0.9
top_speed = 3.0
collide_rate = 0.5
accommodation = 0.8
highest = lax.Precision.HIGHEST
sub = 8
lane = 128
vmem_bytes = 56 * 2**20


def split_table(table):
    high = table.astype(np.float32).astype(jnp.bfloat16)
    low = (table - high.astype(np.float64)).astype(np.float32).astype(jnp.bfloat16)
    return jnp.asarray(high), jnp.asarray(low)


def dft_tables(points):
    half = points // 2
    plane = points * points
    self_modes = [(0, 0), (0, half), (half, 0), (half, half)]
    reps = [(kb, kc) for kb in range(points) for kc in range(1, half)]
    reps += [(kb, 0) for kb in range(1, half)] + [(kb, half) for kb in range(1, half)]
    pairs = [(self_modes[0], self_modes[1]), (self_modes[2], self_modes[3])]
    slots = len(reps) + len(pairs)
    outer, inner = np.divmod(np.arange(plane), points)

    def angle(mode):
        return 2.0 * np.pi / points * ((outer * mode[0] + inner * mode[1]) % points)

    to_modes = np.zeros((plane, plane))
    from_modes = np.zeros((plane, plane))
    for slot, mode in enumerate(reps):
        theta = angle(mode)
        to_modes[:, slot] = np.cos(theta)
        to_modes[:, slots + slot] = -np.sin(theta)
        from_modes[slot] = 2.0 * np.cos(theta)
        from_modes[slots + slot] = -2.0 * np.sin(theta)
    for slot, (first, second) in enumerate(pairs, len(reps)):
        to_modes[:, slot] = from_modes[slot] = np.cos(angle(first))
        to_modes[:, slots + slot] = from_modes[slots + slot] = np.cos(angle(second))
    from_modes /= points * plane
    line = np.arange(points)
    theta = 2.0 * np.pi / points * (line[:, None] * line[None, :] % points)
    forward = np.block([[np.cos(theta), np.sin(theta)], [-np.sin(theta), np.cos(theta)]])
    forward = np.kron(forward, np.eye(sub))

    pick = np.zeros((2, plane, slots + lane), np.float32)

    def add(mode, column, weight):
        kb, kc = mode
        pick[0, kb * points + kc, column] += 0.5 * weight
        pick[1, -kb % points * points + -kc % points, column] += 0.5 * weight

    for slot, mode in enumerate(reps):
        add(mode, slot, 1.0)
    for slot, (first, second) in enumerate(pairs, len(reps)):
        add(first, slot, 0.5)
        add(second, slot, 0.5)
        add(first, slot + lane, 0.5)
        add(second, slot + lane, -0.5)
    return {
        "to_modes": split_table(to_modes),
        "from_modes": split_table(from_modes),
        "forward": split_table(forward),
        "backward": split_table(forward.T),
        "pick": jnp.asarray(pick.astype(jnp.bfloat16)),
    }


def split(values):
    high = values.astype(jnp.bfloat16)
    return high, (values - high.astype(jnp.float32)).astype(jnp.bfloat16)


def dot(a, b):
    return jnp.dot(a, b, preferred_element_type=jnp.float32)


def multiplier_kernel(gain, freq, pick, gain_out, freq_out):
    points = gain.shape[0]
    rows = jnp.concatenate([gain[...], freq[...]], axis=0)
    high, _ = split(rows)
    mid, low = split(rows - high.astype(jnp.float32))
    here, mirrored = (dot(low, pick[i]) + dot(mid, pick[i]) + dot(high, pick[i]) for i in range(2))
    for index, out in enumerate((gain_out, freq_out)):
        for a in range(points):
            at, turned = index * points + a, index * points + -a % points
            row = here[at : at + 1] + mirrored[turned : turned + 1]
            out[a * sub : (a + 1) * sub, :] = jnp.broadcast_to(row, (sub, row.shape[1]))


def multipliers(gain_spectrum, freq_spectrum, pick):
    points = gain_spectrum.shape[0]
    out = jax.ShapeDtypeStruct((points * sub, pick.shape[2]), jnp.float32)
    return pl.pallas_call(
        multiplier_kernel,
        in_specs=[local(pltpu.VMEM)] * 3,
        out_specs=[local(pltpu.VMEM)] * 2,
        out_shape=[out, out],
        compiler_params=pltpu.CompilerParams(vmem_limit_bytes=vmem_bytes),
        cost_estimate=pl.CostEstimate(flops=24 * points * pick.size, bytes_accessed=2 * pick.size, transcendentals=0),
    )(gain_spectrum.reshape(points, -1), freq_spectrum.reshape(points, -1), pick)


def partners(count):
    far = tuple(range(count // 2, count))
    return far, tuple(sorted(range(1, count // 2), key=lambda step: (-step.bit_length(), step)))


def swap(values, axis, step):
    return lax.ppermute(values, axis, [(i, i ^ step) for i in range(lax.axis_size(axis))])


def local(array):
    return pl.BlockSpec(memory_space=array)


def start_of(group, cells, low_groups, gap):
    return pl.multiple_of(group * cells + jnp.where(group < low_groups, 0, gap), sub)


def move_kernel(order, offset, low_groups, gap, points, has_halo, has_after, has_edges, me, particles, *rest):
    count = len(order)
    low, high = rest[:2] if has_halo else (None, None)
    outs = rest[2 * has_halo + has_after :][:count]
    edges = rest[2 * has_halo + has_after + count :][: 2 * has_edges]
    inside, made, rim, in_sems, out_sems = rest[-5:]
    cells, width = outs[0].shape
    total = particles.shape[0]
    planes = width // points**2
    span = inside.shape[1]
    at = me[0]

    def place(step):
        first = offset + start_of(at ^ step, cells, low_groups, gap)
        begin = pl.multiple_of(jnp.clip(first - sub, 0, total - span), sub)
        return first, begin

    def fetch(k, step):
        return pltpu.make_async_copy(particles.at[pl.ds(place(step)[1], span)], inside.at[k], in_sems.at[k])

    def store(k):
        return pltpu.make_async_copy(made.at[k], outs[k], out_sems.at[k])

    def edge_in(k):
        rows = pl.ds((total - sub) * k, sub)
        return pltpu.make_async_copy(particles.at[rows], rim.at[k], in_sems.at[count + k])

    def edge_out(k):
        return pltpu.make_async_copy(rim.at[k], edges[k], out_sems.at[count + k])

    for k, step in enumerate(order):
        fetch(k, step).start()
    for k in range(len(edges)):
        edge_in(k).start()
    for k, step in enumerate(order):
        fetch(k, step).wait()
        first, begin = place(step)
        skip = pl.multiple_of(first - begin, sub)
        ahead = pl.multiple_of(jnp.maximum(skip - sub, 0), sub)
        behind = pl.multiple_of(jnp.minimum(skip + cells, span - sub), sub)
        for plane in range(planes):
            columns = slice(plane * points**2, (plane + 1) * points**2)
            nu = courant * (2 * (at * planes + plane) + 1 - points).astype(jnp.float32) / points
            here = inside[k, pl.ds(skip, cells), columns]
            before = inside[k, pl.ds(ahead, sub), columns][sub - 1 :, :]
            after = inside[k, pl.ds(behind, sub), columns][:1, :]
            if has_halo:
                before = jnp.where(first == 0, low[sub - 1 :, columns], before)
                after = jnp.where(first + cells == total, high[:1, columns], after)
            row = lax.broadcasted_iota(jnp.int32, here.shape, 0)
            left = jnp.where(row == 0, before, pltpu.roll(here, 1, 0))
            right = jnp.where(row == cells - 1, after, pltpu.roll(here, cells - 1, 0))
            made[k, :, columns] = here - nu * jnp.where(nu > 0, here - left, right - here)
        store(k).start()
    for k in range(len(edges)):
        edge_in(k).wait()
        edge_out(k).start()
    for k in range(len(edges)):
        edge_out(k).wait()
    for k in range(count):
        store(k).wait()


def move(me, particles, order, cells, offset, low_groups, gap, points, halo=(), after=(), edges=False):
    total, width = particles.shape
    count = len(order)
    span = min(cells + 2 * sub, total)
    size = count * cells * width
    shape = jax.ShapeDtypeStruct((cells, width), jnp.float32)
    rim = jax.ShapeDtypeStruct((sub, width), jnp.float32)
    flags = (bool(halo), len(after), edges)
    return pl.pallas_call(
        functools.partial(move_kernel, order, offset, low_groups, gap, points, *flags),
        in_specs=[local(pltpu.SMEM), local(pltpu.HBM)]
        + [local(pltpu.VMEM)] * len(halo)
        + [local(pltpu.HBM)] * len(after),
        out_specs=[local(pltpu.HBM)] * (count + 2 * edges),
        out_shape=[shape] * count + [rim] * (2 * edges),
        scratch_shapes=[
            pltpu.VMEM((count, span, width), jnp.float32),
            pltpu.VMEM((count, cells, width), jnp.float32),
            pltpu.VMEM((2, sub, width), jnp.float32),
            pltpu.SemaphoreType.DMA((count + 2,)),
            pltpu.SemaphoreType.DMA((count + 2,)),
        ],
        compiler_params=pltpu.CompilerParams(vmem_limit_bytes=vmem_bytes),
        cost_estimate=pl.CostEstimate(flops=5 * size, bytes_accessed=10 * size, transcendentals=0),
    )(me, particles, *halo, *after)


def collide_kernel(steps, me, *rest):
    count = len(steps)
    xs, rest = rest[:count], rest[count:]
    to_high, to_low, from_high, from_low, ahead_high, ahead_low, back_high, back_low, gain, freq = rest[:10]
    outs, rest = rest[10 : 10 + count], rest[10 + count :]
    mass, wide_high, wide_low, mid, both_high, both_low, fields = rest
    cells, width = xs[0].shape
    plane = to_high.shape[0]
    slots = plane // 2
    planes = width // plane
    points = count * planes
    groups = cells // sub
    chunk = points * sub
    tile = min(256, plane)
    at = me[0]

    def pieces():
        for k, step in enumerate(steps):
            for group in range(groups):
                for j in range(planes):
                    start = (group * points + (at ^ step) * planes + j) * sub
                    here = (slice(group * sub, (group + 1) * sub), slice(j * plane, (j + 1) * plane))
                    yield k, group, here, pl.multiple_of(start, sub)

    for k, group, here, start in pieces():
        mid[pl.ds(start, sub), :] = xs[k][here]
    high, low = split(mid[...])
    wide_high[: groups * chunk, :] = high
    wide_low[: groups * chunk, :] = low

    @pl.loop(0, plane // tile)
    def _(at):
        columns = pl.ds(pl.multiple_of(at * tile, tile), tile)
        table = to_high[:, columns]
        mid[:, columns] = (
            dot(wide_low[: groups * chunk, :], table)
            + dot(wide_high[: groups * chunk, :], to_low[:, columns])
            + dot(wide_high[: groups * chunk, :], table)
        )

    @pl.loop(0, groups)
    def _(group):
        rows = pl.ds(pl.multiple_of(group * chunk, chunk), chunk)
        spectrum = jnp.concatenate([mid[rows, :slots], mid[rows, slots:]], axis=0)
        high, low = split(spectrum)
        waves = dot(ahead_high[...], low) + dot(ahead_low[...], high) + dot(ahead_high[...], high)
        real, imag = waves[:chunk], waves[chunk:]

        def mirror(values):
            tail = values[:, slots - lane :]
            turned = [tail[-a % points * sub : (-a % points + 1) * sub] for a in range(points)]
            return jnp.concatenate(turned, axis=0)

        real_tail, imag_tail = mirror(real), mirror(imag)
        for index, table in enumerate((gain, freq)):
            pad = jnp.zeros((chunk, slots - lane), jnp.float32)
            extra = table[:, slots:]
            upper = real * table[:, :slots] + jnp.concatenate([pad, real_tail * extra], axis=1)
            lower = imag * table[:, :slots] - jnp.concatenate([pad, imag_tail * extra], axis=1)
            for start, values in ((0, upper), (chunk, lower)):
                high, low = split(values)
                both_high[start : start + chunk, index * slots : (index + 1) * slots] = high
                both_low[start : start + chunk, index * slots : (index + 1) * slots] = low
        for index in range(2):
            columns = slice(index * slots, (index + 1) * slots)
            lines = (
                dot(back_high[...], both_low[:, columns])
                + dot(back_low[...], both_high[:, columns])
                + dot(back_high[...], both_high[:, columns])
            )
            high, low = split(jnp.concatenate([lines[:chunk], lines[chunk:]], axis=1))
            at = pl.ds(pl.multiple_of((index * groups + group) * chunk, chunk), chunk)
            wide_high[at, :] = high
            wide_low[at, :] = low

    @pl.loop(0, plane // tile)
    def _(at):
        columns = pl.ds(pl.multiple_of(at * tile, tile), tile)
        table = from_high[:, columns]
        fields[:, columns] = (
            dot(wide_low[...], table) + dot(wide_high[...], from_low[:, columns]) + dot(wide_high[...], table)
        )

    totals = [jnp.zeros((sub, plane), jnp.float32)] * groups
    for k, group, here, start in pieces():
        cube = xs[k][here]
        gained = fields[pl.ds(start, sub), :]
        lost = fields[pl.ds(pl.multiple_of(groups * chunk + start, sub), sub), :]
        post = cube + collide_rate * (gained - cube * lost)
        outs[k][here] = post
        totals[group] = totals[group] + post
    for group, total in enumerate(totals):
        lanes = total[:, :lane]
        for column in range(lane, plane, lane):
            lanes = lanes + total[:, column : column + lane]
        mass[group * sub : (group + 1) * sub, :] = lanes


def collide(me, cubes, steps, tables, gain, freq):
    cells, width = cubes[0].shape
    count = len(cubes)
    plane = tables["to_modes"][0].shape[0]
    points = count * width // plane
    step = math.gcd(cells, 2 * sub)
    chunk = step * points
    operands = [*tables["to_modes"], *tables["from_modes"], *tables["forward"], *tables["backward"], gain, freq]
    bf16, f32 = jnp.bfloat16, jnp.float32
    block = pl.BlockSpec((step, width), lambda i: (i, 0))
    multiply_adds = 3 * cells * points * (3 * plane * plane + 6 * points * sub * plane)
    *posts, mass = pl.pallas_call(
        functools.partial(collide_kernel, steps),
        grid=(cells // step,),
        in_specs=[local(pltpu.SMEM)] + [block] * count + [local(pltpu.VMEM)] * len(operands),
        out_specs=[block] * count + [pl.BlockSpec((step, lane), lambda i: (i, 0))],
        out_shape=[jax.ShapeDtypeStruct((cells, width), f32)] * count + [jax.ShapeDtypeStruct((cells, lane), f32)],
        scratch_shapes=[
            pltpu.VMEM((2 * chunk, plane), bf16),
            pltpu.VMEM((2 * chunk, plane), bf16),
            pltpu.VMEM((chunk, plane), f32),
            pltpu.VMEM((2 * points * sub, plane), bf16),
            pltpu.VMEM((2 * points * sub, plane), bf16),
            pltpu.VMEM((2 * chunk, plane), f32),
        ],
        compiler_params=pltpu.CompilerParams(vmem_limit_bytes=vmem_bytes),
        cost_estimate=pl.CostEstimate(
            flops=3 * multiply_adds, bytes_accessed=8 * count * cells * width, transcendentals=0
        ),
    )(me, *cubes, *operands)
    return posts, mass


def mass_kernel(count, *refs):
    parts, out = refs[:count], refs[-1]
    total = jnp.zeros(out.shape, jnp.float32)
    for mass, member in zip(parts[::2], parts[1::2]):
        cell = jnp.sum(mass[...], axis=1, keepdims=True)
        total = total + jnp.sum(member[...] * cell, axis=0, keepdims=True)
    out[...] = total


def panel_mass(pairs, after):
    flat = [array for pair in pairs for array in pair]
    return pl.pallas_call(
        functools.partial(mass_kernel, len(flat)),
        in_specs=[local(pltpu.VMEM)] * len(flat) + [local(pl.ANY)] * len(after),
        out_specs=local(pltpu.VMEM),
        out_shape=jax.ShapeDtypeStruct((1, flat[1].shape[1]), jnp.float32),
    )(*flat, *after)


def settle_kernel(steps, offset, low_groups, gap, me, member, emit, *rest):
    count = len(steps)
    posts = rest[:count]
    out, held, emission, in_sems, out_sems = rest[-5:]
    cells, width = held.shape[1:]
    at = me[0]

    def fetch(k):
        return pltpu.make_async_copy(posts[k], held.at[k], in_sems.at[k])

    def store(k):
        first = offset + start_of(at ^ steps[k], cells, low_groups, gap)
        return pltpu.make_async_copy(held.at[k], out.at[pl.ds(first, cells)], out_sems.at[k])

    for k in range(count):
        fetch(k).start()
    chosen = member[...]
    share = accommodation * jnp.sum(chosen, axis=1, keepdims=True)
    emission[...] = dot(jnp.concatenate([chosen, chosen], axis=1).astype(jnp.bfloat16), emit[...])
    for k in range(count):
        fetch(k).wait()
        rows = pl.ds(pl.multiple_of(k * cells, sub), cells)
        post = held[k]
        held[k] = post + (accommodation * emission[rows, :] - share[k * cells : (k + 1) * cells] * post)
        store(k).start()
    for k in range(count):
        store(k).wait()


def settle(me, posts, steps, member, emit, earlier, shape, offset, low_groups, gap):
    cells, width = posts[0].shape
    count = len(posts)
    size = count * cells * width
    operands = [me, member, emit, *posts]
    in_specs = [local(pltpu.SMEM), local(pltpu.VMEM), local(pltpu.VMEM)] + [local(pl.ANY)] * count
    aliases = {}
    if earlier is not None:
        aliases = {len(operands): 0}
        operands.append(earlier)
        in_specs.append(local(pltpu.HBM))
    return pl.pallas_call(
        functools.partial(settle_kernel, steps, offset, low_groups, gap),
        in_specs=in_specs,
        out_specs=local(pltpu.HBM),
        out_shape=jax.ShapeDtypeStruct(shape, jnp.float32),
        scratch_shapes=[
            pltpu.VMEM((count, cells, width), jnp.float32),
            pltpu.VMEM((count * cells, width), jnp.float32),
            pltpu.SemaphoreType.DMA((count,)),
            pltpu.SemaphoreType.DMA((count,)),
        ],
        input_output_aliases=aliases,
        compiler_params=pltpu.CompilerParams(vmem_limit_bytes=vmem_bytes),
        cost_estimate=pl.CostEstimate(
            flops=4 * member.shape[1] * size, bytes_accessed=8 * size, transcendentals=0
        ),
    )(*operands)


def on_device(particles, gain_spectrum, freq_spectrum, panel_temp, wall_cells):
    cell_dev, vel_dev = particles.shape
    points = gain_spectrum.shape[0]
    plane_size = points * points
    planes = vel_dev // plane_size
    vel_count = lax.axis_size("vel")
    vel_at = lax.axis_index("vel")
    space_at = lax.axis_index("space")
    space_count = lax.axis_size("space")
    me = vel_at.astype(jnp.int32)[None]
    tables = dft_tables(points)
    panels, per_panel = wall_cells.shape

    quarter, half = cell_dev // 4, cell_dev // 2
    cells = half // vel_count
    inner, outer = (quarter, vel_count, 0), (0, vel_count // 2, half)
    far, near = partners(vel_count)
    steps = (*far, *near, 0)
    urgent, ready = far[:2], (*far, *near[:1])

    def send(arrays):
        return {step: swap(array, "vel", step) if step else array for step, array in arrays.items()}

    def rest(done):
        return tuple(step for step in steps if step not in done)

    early = move(me, particles, urgent, cells, *inner, points)
    *late, first_rows, last_rows = move(
        me, particles, rest(urgent), cells, *inner, points, after=early[:1], edges=True
    )
    inner_moved = dict(zip((*urgent, *rest(urgent)), (*early, *late)))
    inner_cubes = send({step: inner_moved[step] for step in far})
    behind, ahead = near, far[:1]
    tied = lax.optimization_barrier(tuple(inner_moved[step] for step in behind) + tuple(inner_cubes[step] for step in ahead))
    inner_moved.update(zip(behind, tied))
    inner_cubes.update(zip(ahead, tied[len(behind) :]))
    inner_cubes.update(send({step: inner_moved[step] for step in (*near, 0)}))
    space_pairs = [(i, i + 1) for i in range(space_count - 1)]
    low = lax.ppermute(last_rows, "space", space_pairs)
    high = lax.ppermute(first_rows, "space", [(target, source) for source, target in space_pairs])
    outer_early = move(me, particles, ready, cells, *outer, points, halo=(low, high))
    gain, freq = multipliers(gain_spectrum, freq_spectrum, tables["pick"])

    def collided(cubes):
        posts, mass = collide(me, [cubes[step] for step in steps], steps, tables, gain, freq)
        return dict(zip(steps, posts)), mass

    inner_posts, inner_mass = collided(inner_cubes)
    outer_late = move(
        me, particles, rest(ready), cells, *outer, points, halo=(low, high), after=(inner_mass,)
    )
    outer_cubes = send(dict(zip((*ready, *rest(ready)), (*outer_early, *outer_late))))
    outer_posts, outer_mass = collided(outer_cubes)

    def cells_of(plan, group):
        offset, low_groups, gap = plan
        first = offset + group * cells + jnp.where(group < low_groups, 0, gap)
        return space_at * cell_dev + first + jnp.arange(cells, dtype=jnp.int32)

    def membership(cell_ids):
        hit = wall_cells.reshape(1, panels, per_panel) == cell_ids[:, None, None]
        return jnp.any(hit, axis=2).astype(jnp.float32)

    held = near
    *tied, outer_mass = lax.optimization_barrier((*(inner_posts[step] for step in held), outer_mass))
    inner_back = send({**inner_posts, **dict(zip(held, tied))})
    outer_back = send(outer_posts)
    pairs = [
        (mass, membership(cells_of(plan, vel_at))) for mass, plan in ((inner_mass, inner), (outer_mass, outer))
    ]
    wall_mass = lax.psum(panel_mass(pairs, [inner_back[step] for step in (*far, *near)]), "space")
    step = 1
    while step < vel_count:
        wall_mass = wall_mass + swap(wall_mass, "vel", step)
        step *= 2

    def speed(index):
        return top_speed * (2 * index + 1 - points).astype(jnp.float32) / points

    line = jnp.arange(points, dtype=jnp.int32)
    line_weight = jnp.exp(-(speed(line) ** 2)[None, :] / (2.0 * panel_temp[:, None]))
    normal_sum = jnp.sum(line_weight, axis=1) ** 3
    columns = jnp.arange(vel_dev, dtype=jnp.int32)
    plane_index = vel_at * planes + columns // plane_size
    speed_sq = speed(plane_index) ** 2 + speed(columns // points % points) ** 2 + speed(columns % points) ** 2
    profile = jnp.exp(-speed_sq[None, :] / (2.0 * panel_temp[:, None]))
    maxwellian = profile / normal_sum[:, None]
    emission = (wall_mass.reshape(panels, 1) / per_panel) * maxwellian
    emit_high = lax.reduce_precision(emission, exponent_bits=8, mantissa_bits=7)
    emit = jnp.concatenate([emit_high, emission - emit_high], axis=0).astype(jnp.bfloat16)

    def wall(posts, part, plan, earlier):
        ids = jnp.concatenate([cells_of(plan, vel_at ^ step) for step in part])
        posts = [posts[step] for step in part]
        return settle(me, posts, part, membership(ids), emit, earlier, particles.shape, *plan)

    out = wall(inner_back, steps, inner, None)
    return wall(outer_back, (*far[:2], near[0], far[2], *near[1:], *far[3:], 0), outer, out)


def solution(mesh):
    in_specs = (P("space", "vel"), P(), P(), P(), P())
    out_specs = P("space", "vel")
    return jax.shard_map(on_device, mesh=mesh, in_specs=in_specs, out_specs=out_specs, check_vma=False)
```

```python
import functools
import math

import jax
import jax.numpy as jnp
import numpy as np
from jax import lax
from jax.experimental import pallas as pl
from jax.experimental.pallas import tpu as pltpu
from jax.sharding import PartitionSpec as P

courant = 0.9
top_speed = 3.0
collide_rate = 0.5
accommodation = 0.8
highest = lax.Precision.HIGHEST
sub = 8
lane = 128
vmem_bytes = 56 * 2**20


def split_table(table):
    high = table.astype(np.float32).astype(jnp.bfloat16)
    low = (table - high.astype(np.float64)).astype(np.float32).astype(jnp.bfloat16)
    return jnp.asarray(high), jnp.asarray(low)


def dft_tables(points):
    half = points // 2
    plane = points * points
    self_modes = [(0, 0), (0, half), (half, 0), (half, half)]
    reps = [(kb, kc) for kb in range(points) for kc in range(1, half)]
    reps += [(kb, 0) for kb in range(1, half)] + [(kb, half) for kb in range(1, half)]
    pairs = [(self_modes[0], self_modes[1]), (self_modes[2], self_modes[3])]
    slots = len(reps) + len(pairs)
    outer, inner = np.divmod(np.arange(plane), points)

    def angle(mode):
        return 2.0 * np.pi / points * ((outer * mode[0] + inner * mode[1]) % points)

    to_modes = np.zeros((plane, plane))
    from_modes = np.zeros((plane, plane))
    for slot, mode in enumerate(reps):
        theta = angle(mode)
        to_modes[:, slot] = np.cos(theta)
        to_modes[:, slots + slot] = -np.sin(theta)
        from_modes[slot] = 2.0 * np.cos(theta)
        from_modes[slots + slot] = -2.0 * np.sin(theta)
    for slot, (first, second) in enumerate(pairs, len(reps)):
        to_modes[:, slot] = from_modes[slot] = np.cos(angle(first))
        to_modes[:, slots + slot] = from_modes[slots + slot] = np.cos(angle(second))
    from_modes /= points * plane
    line = np.arange(points)
    theta = 2.0 * np.pi / points * (line[:, None] * line[None, :] % points)
    forward = np.block([[np.cos(theta), np.sin(theta)], [-np.sin(theta), np.cos(theta)]])
    forward = np.kron(forward, np.eye(sub))

    pick = np.zeros((2, plane, slots + lane), np.float32)

    def add(mode, column, weight):
        kb, kc = mode
        pick[0, kb * points + kc, column] += 0.5 * weight
        pick[1, -kb % points * points + -kc % points, column] += 0.5 * weight

    for slot, mode in enumerate(reps):
        add(mode, slot, 1.0)
    for slot, (first, second) in enumerate(pairs, len(reps)):
        add(first, slot, 0.5)
        add(second, slot, 0.5)
        add(first, slot + lane, 0.5)
        add(second, slot + lane, -0.5)
    return {
        "to_modes": split_table(to_modes),
        "from_modes": split_table(from_modes),
        "forward": split_table(forward),
        "backward": split_table(forward.T),
        "pick": jnp.asarray(pick.astype(jnp.bfloat16)),
    }


def split(values):
    high = values.astype(jnp.bfloat16)
    return high, (values - high.astype(jnp.float32)).astype(jnp.bfloat16)


def dot(a, b):
    return jnp.dot(a, b, preferred_element_type=jnp.float32)


def multiplier_kernel(gain, freq, pick, gain_out, freq_out):
    points = gain.shape[0]
    rows = jnp.concatenate([gain[...], freq[...]], axis=0)
    high, _ = split(rows)
    mid, low = split(rows - high.astype(jnp.float32))
    here, mirrored = (dot(low, pick[i]) + dot(mid, pick[i]) + dot(high, pick[i]) for i in range(2))
    for index, out in enumerate((gain_out, freq_out)):
        for a in range(points):
            at, turned = index * points + a, index * points + -a % points
            row = here[at : at + 1] + mirrored[turned : turned + 1]
            out[a * sub : (a + 1) * sub, :] = jnp.broadcast_to(row, (sub, row.shape[1]))


def multipliers(gain_spectrum, freq_spectrum, pick):
    points = gain_spectrum.shape[0]
    out = jax.ShapeDtypeStruct((points * sub, pick.shape[2]), jnp.float32)
    return pl.pallas_call(
        multiplier_kernel,
        in_specs=[local(pltpu.VMEM)] * 3,
        out_specs=[local(pltpu.VMEM)] * 2,
        out_shape=[out, out],
        compiler_params=pltpu.CompilerParams(vmem_limit_bytes=vmem_bytes),
        cost_estimate=pl.CostEstimate(flops=24 * points * pick.size, bytes_accessed=2 * pick.size, transcendentals=0),
    )(gain_spectrum.reshape(points, -1), freq_spectrum.reshape(points, -1), pick)


def partners(count):
    far = tuple(range(count // 2, count))
    return far, tuple(sorted(range(1, count // 2), key=lambda step: (-step.bit_length(), step)))


def swap(values, axis, step):
    return lax.ppermute(values, axis, [(i, i ^ step) for i in range(lax.axis_size(axis))])


def local(array):
    return pl.BlockSpec(memory_space=array)


def start_of(group, cells, low_groups, gap):
    return pl.multiple_of(group * cells + jnp.where(group < low_groups, 0, gap), sub)


def move_kernel(order, offset, low_groups, gap, points, has_halo, has_after, has_edges, me, particles, *rest):
    count = len(order)
    low, high = rest[:2] if has_halo else (None, None)
    outs = rest[2 * has_halo + has_after :][:count]
    edges = rest[2 * has_halo + has_after + count :][: 2 * has_edges]
    inside, made, rim, in_sems, out_sems = rest[-5:]
    cells, width = outs[0].shape
    total = particles.shape[0]
    planes = width // points**2
    span = inside.shape[1]
    at = me[0]

    def place(step):
        first = offset + start_of(at ^ step, cells, low_groups, gap)
        begin = pl.multiple_of(jnp.clip(first - sub, 0, total - span), sub)
        return first, begin

    def fetch(k, step):
        return pltpu.make_async_copy(particles.at[pl.ds(place(step)[1], span)], inside.at[k], in_sems.at[k])

    def store(k):
        return pltpu.make_async_copy(made.at[k], outs[k], out_sems.at[k])

    def edge_in(k):
        rows = pl.ds((total - sub) * k, sub)
        return pltpu.make_async_copy(particles.at[rows], rim.at[k], in_sems.at[count + k])

    def edge_out(k):
        return pltpu.make_async_copy(rim.at[k], edges[k], out_sems.at[count + k])

    for k, step in enumerate(order):
        fetch(k, step).start()
    for k in range(len(edges)):
        edge_in(k).start()
    for k, step in enumerate(order):
        fetch(k, step).wait()
        first, begin = place(step)
        skip = pl.multiple_of(first - begin, sub)
        ahead = pl.multiple_of(jnp.maximum(skip - sub, 0), sub)
        behind = pl.multiple_of(jnp.minimum(skip + cells, span - sub), sub)
        for plane in range(planes):
            columns = slice(plane * points**2, (plane + 1) * points**2)
            nu = courant * (2 * (at * planes + plane) + 1 - points).astype(jnp.float32) / points
            here = inside[k, pl.ds(skip, cells), columns]
            before = inside[k, pl.ds(ahead, sub), columns][sub - 1 :, :]
            after = inside[k, pl.ds(behind, sub), columns][:1, :]
            if has_halo:
                before = jnp.where(first == 0, low[sub - 1 :, columns], before)
                after = jnp.where(first + cells == total, high[:1, columns], after)
            row = lax.broadcasted_iota(jnp.int32, here.shape, 0)
            left = jnp.where(row == 0, before, pltpu.roll(here, 1, 0))
            right = jnp.where(row == cells - 1, after, pltpu.roll(here, cells - 1, 0))
            made[k, :, columns] = here - nu * jnp.where(nu > 0, here - left, right - here)
        store(k).start()
    for k in range(len(edges)):
        edge_in(k).wait()
        edge_out(k).start()
    for k in range(len(edges)):
        edge_out(k).wait()
    for k in range(count):
        store(k).wait()


def move(me, particles, order, cells, offset, low_groups, gap, points, halo=(), after=(), edges=False):
    total, width = particles.shape
    count = len(order)
    span = min(cells + 2 * sub, total)
    size = count * cells * width
    shape = jax.ShapeDtypeStruct((cells, width), jnp.float32)
    rim = jax.ShapeDtypeStruct((sub, width), jnp.float32)
    flags = (bool(halo), len(after), edges)
    return pl.pallas_call(
        functools.partial(move_kernel, order, offset, low_groups, gap, points, *flags),
        in_specs=[local(pltpu.SMEM), local(pltpu.HBM)]
        + [local(pltpu.VMEM)] * len(halo)
        + [local(pltpu.HBM)] * len(after),
        out_specs=[local(pltpu.HBM)] * (count + 2 * edges),
        out_shape=[shape] * count + [rim] * (2 * edges),
        scratch_shapes=[
            pltpu.VMEM((count, span, width), jnp.float32),
            pltpu.VMEM((count, cells, width), jnp.float32),
            pltpu.VMEM((2, sub, width), jnp.float32),
            pltpu.SemaphoreType.DMA((count + 2,)),
            pltpu.SemaphoreType.DMA((count + 2,)),
        ],
        compiler_params=pltpu.CompilerParams(vmem_limit_bytes=vmem_bytes),
        cost_estimate=pl.CostEstimate(flops=5 * size, bytes_accessed=10 * size, transcendentals=0),
    )(me, particles, *halo, *after)


def collide_kernel(steps, me, *rest):
    count = len(steps)
    xs, rest = rest[:count], rest[count:]
    to_high, to_low, from_high, from_low, ahead_high, ahead_low, back_high, back_low, gain, freq = rest[:10]
    outs, rest = rest[10 : 10 + count], rest[10 + count :]
    mass, wide_high, wide_low, mid, both_high, both_low, fields = rest
    cells, width = xs[0].shape
    plane = to_high.shape[0]
    slots = plane // 2
    planes = width // plane
    points = count * planes
    groups = cells // sub
    chunk = points * sub
    tile = min(256, plane)
    at = me[0]

    def pieces():
        for k, step in enumerate(steps):
            for group in range(groups):
                for j in range(planes):
                    start = (group * points + (at ^ step) * planes + j) * sub
                    here = (slice(group * sub, (group + 1) * sub), slice(j * plane, (j + 1) * plane))
                    yield k, group, here, pl.multiple_of(start, sub)

    for k, group, here, start in pieces():
        mid[pl.ds(start, sub), :] = xs[k][here]
    high, low = split(mid[...])
    wide_high[: groups * chunk, :] = high
    wide_low[: groups * chunk, :] = low

    @pl.loop(0, plane // tile)
    def _(at):
        columns = pl.ds(pl.multiple_of(at * tile, tile), tile)
        table = to_high[:, columns]
        mid[:, columns] = (
            dot(wide_low[: groups * chunk, :], table)
            + dot(wide_high[: groups * chunk, :], to_low[:, columns])
            + dot(wide_high[: groups * chunk, :], table)
        )

    @pl.loop(0, groups)
    def _(group):
        rows = pl.ds(pl.multiple_of(group * chunk, chunk), chunk)
        spectrum = jnp.concatenate([mid[rows, :slots], mid[rows, slots:]], axis=0)
        high, low = split(spectrum)
        waves = dot(ahead_high[...], low) + dot(ahead_low[...], high) + dot(ahead_high[...], high)
        real, imag = waves[:chunk], waves[chunk:]

        def mirror(values):
            tail = values[:, slots - lane :]
            turned = [tail[-a % points * sub : (-a % points + 1) * sub] for a in range(points)]
            return jnp.concatenate(turned, axis=0)

        real_tail, imag_tail = mirror(real), mirror(imag)
        for index, table in enumerate((gain, freq)):
            pad = jnp.zeros((chunk, slots - lane), jnp.float32)
            extra = table[:, slots:]
            upper = real * table[:, :slots] + jnp.concatenate([pad, real_tail * extra], axis=1)
            lower = imag * table[:, :slots] - jnp.concatenate([pad, imag_tail * extra], axis=1)
            for start, values in ((0, upper), (chunk, lower)):
                high, low = split(values)
                both_high[start : start + chunk, index * slots : (index + 1) * slots] = high
                both_low[start : start + chunk, index * slots : (index + 1) * slots] = low
        for index in range(2):
            columns = slice(index * slots, (index + 1) * slots)
            lines = (
                dot(back_high[...], both_low[:, columns])
                + dot(back_low[...], both_high[:, columns])
                + dot(back_high[...], both_high[:, columns])
            )
            high, low = split(jnp.concatenate([lines[:chunk], lines[chunk:]], axis=1))
            at = pl.ds(pl.multiple_of((index * groups + group) * chunk, chunk), chunk)
            wide_high[at, :] = high
            wide_low[at, :] = low

    @pl.loop(0, plane // tile)
    def _(at):
        columns = pl.ds(pl.multiple_of(at * tile, tile), tile)
        table = from_high[:, columns]
        fields[:, columns] = (
            dot(wide_low[...], table) + dot(wide_high[...], from_low[:, columns]) + dot(wide_high[...], table)
        )

    totals = [jnp.zeros((sub, plane), jnp.float32)] * groups
    for k, group, here, start in pieces():
        cube = xs[k][here]
        gained = fields[pl.ds(start, sub), :]
        lost = fields[pl.ds(pl.multiple_of(groups * chunk + start, sub), sub), :]
        post = cube + collide_rate * (gained - cube * lost)
        outs[k][here] = post
        totals[group] = totals[group] + post
    for group, total in enumerate(totals):
        lanes = total[:, :lane]
        for column in range(lane, plane, lane):
            lanes = lanes + total[:, column : column + lane]
        mass[group * sub : (group + 1) * sub, :] = lanes


def collide(me, cubes, steps, tables, gain, freq):
    cells, width = cubes[0].shape
    count = len(cubes)
    plane = tables["to_modes"][0].shape[0]
    points = count * width // plane
    step = math.gcd(cells, 2 * sub)
    chunk = step * points
    operands = [*tables["to_modes"], *tables["from_modes"], *tables["forward"], *tables["backward"], gain, freq]
    bf16, f32 = jnp.bfloat16, jnp.float32
    block = pl.BlockSpec((step, width), lambda i: (i, 0))
    multiply_adds = 3 * cells * points * (3 * plane * plane + 6 * points * sub * plane)
    *posts, mass = pl.pallas_call(
        functools.partial(collide_kernel, steps),
        grid=(cells // step,),
        in_specs=[local(pltpu.SMEM)] + [block] * count + [local(pltpu.VMEM)] * len(operands),
        out_specs=[block] * count + [pl.BlockSpec((step, lane), lambda i: (i, 0))],
        out_shape=[jax.ShapeDtypeStruct((cells, width), f32)] * count + [jax.ShapeDtypeStruct((cells, lane), f32)],
        scratch_shapes=[
            pltpu.VMEM((2 * chunk, plane), bf16),
            pltpu.VMEM((2 * chunk, plane), bf16),
            pltpu.VMEM((chunk, plane), f32),
            pltpu.VMEM((2 * points * sub, plane), bf16),
            pltpu.VMEM((2 * points * sub, plane), bf16),
            pltpu.VMEM((2 * chunk, plane), f32),
        ],
        compiler_params=pltpu.CompilerParams(vmem_limit_bytes=vmem_bytes),
        cost_estimate=pl.CostEstimate(
            flops=3 * multiply_adds, bytes_accessed=8 * count * cells * width, transcendentals=0
        ),
    )(me, *cubes, *operands)
    return posts, mass


def mass_kernel(count, *refs):
    parts, out = refs[:count], refs[-1]
    total = jnp.zeros(out.shape, jnp.float32)
    for mass, member in zip(parts[::2], parts[1::2]):
        cell = jnp.sum(mass[...], axis=1, keepdims=True)
        total = total + jnp.sum(member[...] * cell, axis=0, keepdims=True)
    out[...] = total


def panel_mass(pairs, after):
    flat = [array for pair in pairs for array in pair]
    return pl.pallas_call(
        functools.partial(mass_kernel, len(flat)),
        in_specs=[local(pltpu.VMEM)] * len(flat) + [local(pl.ANY)] * len(after),
        out_specs=local(pltpu.VMEM),
        out_shape=jax.ShapeDtypeStruct((1, flat[1].shape[1]), jnp.float32),
    )(*flat, *after)


def settle_kernel(groups, me, member, emit, *rest):
    count = len(groups)
    posts = rest[:count]
    out, held, emission, in_sems, out_sems = rest[-5:]
    cells = held.shape[1]
    at = me[0]

    def fetch(k):
        return pltpu.make_async_copy(posts[k], held.at[k], in_sems.at[k])

    def store(k):
        step, (offset, low_groups, gap) = groups[k]
        first = offset + start_of(at ^ step, cells, low_groups, gap)
        return pltpu.make_async_copy(held.at[k], out.at[pl.ds(first, cells)], out_sems.at[k])

    for k in range(count):
        fetch(k).start()
    chosen = member[...]
    share = accommodation * jnp.sum(chosen, axis=1, keepdims=True)
    emission[...] = dot(jnp.concatenate([chosen, chosen], axis=1).astype(jnp.bfloat16), emit[...])
    for k in range(count):
        fetch(k).wait()
        rows = slice(k * cells, (k + 1) * cells)
        post = held[k]
        held[k] = post + (accommodation * emission[rows, :] - share[rows] * post)
        store(k).start()
    for k in range(count):
        store(k).wait()


def settle(me, posts, groups, member, emit, earlier, shape):
    cells, width = posts[0].shape
    count = len(posts)
    size = count * cells * width
    operands = [me, member, emit, *posts]
    in_specs = [local(pltpu.SMEM), local(pltpu.VMEM), local(pltpu.VMEM)] + [local(pl.ANY)] * count
    aliases = {}
    if earlier is not None:
        aliases = {len(operands): 0}
        operands.append(earlier)
        in_specs.append(local(pltpu.HBM))
    return pl.pallas_call(
        functools.partial(settle_kernel, groups),
        in_specs=in_specs,
        out_specs=local(pltpu.HBM),
        out_shape=jax.ShapeDtypeStruct(shape, jnp.float32),
        scratch_shapes=[
            pltpu.VMEM((count, cells, width), jnp.float32),
            pltpu.VMEM((count * cells, width), jnp.float32),
            pltpu.SemaphoreType.DMA((count,)),
            pltpu.SemaphoreType.DMA((count,)),
        ],
        input_output_aliases=aliases,
        compiler_params=pltpu.CompilerParams(vmem_limit_bytes=8 * size + 6 * 2**20),
        cost_estimate=pl.CostEstimate(
            flops=4 * member.shape[1] * size, bytes_accessed=8 * size, transcendentals=0
        ),
    )(*operands)


def on_device(particles, gain_spectrum, freq_spectrum, panel_temp, wall_cells):
    cell_dev, vel_dev = particles.shape
    points = gain_spectrum.shape[0]
    plane_size = points * points
    planes = vel_dev // plane_size
    vel_count = lax.axis_size("vel")
    vel_at = lax.axis_index("vel")
    space_at = lax.axis_index("space")
    space_count = lax.axis_size("space")
    me = vel_at.astype(jnp.int32)[None]
    tables = dft_tables(points)
    panels, per_panel = wall_cells.shape

    quarter, half = cell_dev // 4, cell_dev // 2
    cells = half // vel_count
    inner, outer = (quarter, vel_count, 0), (0, vel_count // 2, half)
    far, near = partners(vel_count)
    steps = (*far, *near, 0)
    urgent, ready = far[:1], (*far, *near[:1])

    def send(arrays):
        return {step: swap(array, "vel", step) if step else array for step, array in arrays.items()}

    def rest(done):
        return tuple(step for step in steps if step not in done)

    early = move(me, particles, urgent, cells, *inner, points)
    *late, first_rows, last_rows = move(
        me, particles, rest(urgent), cells, *inner, points, after=early[:1], edges=True
    )
    inner_moved = dict(zip((*urgent, *rest(urgent)), (*early, *late)))
    inner_cubes = send({step: inner_moved[step] for step in far})
    behind, ahead = near, far[:1]
    tied = lax.optimization_barrier(tuple(inner_moved[step] for step in behind) + tuple(inner_cubes[step] for step in ahead))
    inner_moved.update(zip(behind, tied))
    inner_cubes.update(zip(ahead, tied[len(behind) :]))
    inner_cubes.update(send({step: inner_moved[step] for step in (*near, 0)}))
    space_pairs = [(i, i + 1) for i in range(space_count - 1)]
    low = lax.ppermute(last_rows, "space", space_pairs)
    high = lax.ppermute(first_rows, "space", [(target, source) for source, target in space_pairs])
    outer_early = move(me, particles, ready, cells, *outer, points, halo=(low, high))
    gain, freq = multipliers(gain_spectrum, freq_spectrum, tables["pick"])

    def collided(cubes):
        posts, mass = collide(me, [cubes[step] for step in steps], steps, tables, gain, freq)
        return dict(zip(steps, posts)), mass

    inner_posts, inner_mass = collided(inner_cubes)
    outer_late = move(
        me, particles, rest(ready), cells, *outer, points, halo=(low, high), after=(inner_mass,)
    )
    outer_cubes = send(dict(zip((*ready, *rest(ready)), (*outer_early, *outer_late))))
    outer_posts, outer_mass = collided(outer_cubes)

    def cells_of(plan, group):
        offset, low_groups, gap = plan
        first = offset + group * cells + jnp.where(group < low_groups, 0, gap)
        return space_at * cell_dev + first + jnp.arange(cells, dtype=jnp.int32)

    def membership(cell_ids):
        hit = wall_cells.reshape(1, panels, per_panel) == cell_ids[:, None, None]
        return jnp.any(hit, axis=2).astype(jnp.float32)

    held = near
    *tied, outer_mass = lax.optimization_barrier((*(inner_posts[step] for step in held), outer_mass))
    inner_back = send({**inner_posts, **dict(zip(held, tied))})
    outer_back = send(outer_posts)
    pairs = [
        (mass, membership(cells_of(plan, vel_at))) for mass, plan in ((inner_mass, inner), (outer_mass, outer))
    ]
    wall_mass = lax.psum(panel_mass(pairs, [inner_back[step] for step in (*far, *near)]), "space")
    step = 1
    while step < vel_count:
        wall_mass = wall_mass + swap(wall_mass, "vel", step)
        step *= 2

    def speed(index):
        return top_speed * (2 * index + 1 - points).astype(jnp.float32) / points

    line = jnp.arange(points, dtype=jnp.int32)
    line_weight = jnp.exp(-(speed(line) ** 2)[None, :] / (2.0 * panel_temp[:, None]))
    normal_sum = jnp.sum(line_weight, axis=1) ** 3
    columns = jnp.arange(vel_dev, dtype=jnp.int32)
    plane_index = vel_at * planes + columns // plane_size
    speed_sq = speed(plane_index) ** 2 + speed(columns // points % points) ** 2 + speed(columns % points) ** 2
    profile = jnp.exp(-speed_sq[None, :] / (2.0 * panel_temp[:, None]))
    maxwellian = profile / normal_sum[:, None]
    emission = (wall_mass.reshape(panels, 1) / per_panel) * maxwellian
    emit_high = lax.reduce_precision(emission, exponent_bits=8, mantissa_bits=7)
    emit = jnp.concatenate([emit_high, emission - emit_high], axis=0).astype(jnp.bfloat16)

    def wall(arrived, earlier):
        groups, posts = zip(*arrived)
        ids = jnp.concatenate([cells_of(plan, vel_at ^ step) for step, plan in groups])
        return settle(me, posts, groups, membership(ids), emit, earlier, particles.shape)

    final = (near[0], far[2], *near[1:], *far[3:])
    first = [((step, inner), inner_back[step]) for step in steps]
    first += [((step, outer), outer_back[step]) for step in rest(final)]
    return wall([((step, outer), outer_back[step]) for step in final], wall(first, None))


def solution(mesh):
    in_specs = (P("space", "vel"), P(), P(), P(), P())
    out_specs = P("space", "vel")
    return jax.shard_map(on_device, mesh=mesh, in_specs=in_specs, out_specs=out_specs, check_vma=False)
```

```python
import functools
import math

import jax
import jax.numpy as jnp
import numpy as np
from jax import lax
from jax.experimental import pallas as pl
from jax.experimental.pallas import tpu as pltpu
from jax.sharding import PartitionSpec as P

courant = 0.9
top_speed = 3.0
collide_rate = 0.5
accommodation = 0.8
highest = lax.Precision.HIGHEST
sub = 8
lane = 128
vmem_bytes = 56 * 2**20


def split_table(table):
    high = table.astype(np.float32).astype(jnp.bfloat16)
    low = (table - high.astype(np.float64)).astype(np.float32).astype(jnp.bfloat16)
    return jnp.asarray(high), jnp.asarray(low)


def dft_tables(points):
    half = points // 2
    plane = points * points
    self_modes = [(0, 0), (0, half), (half, 0), (half, half)]
    reps = [(kb, kc) for kb in range(points) for kc in range(1, half)]
    reps += [(kb, 0) for kb in range(1, half)] + [(kb, half) for kb in range(1, half)]
    pairs = [(self_modes[0], self_modes[1]), (self_modes[2], self_modes[3])]
    slots = len(reps) + len(pairs)
    outer, inner = np.divmod(np.arange(plane), points)

    def angle(mode):
        return 2.0 * np.pi / points * ((outer * mode[0] + inner * mode[1]) % points)

    to_modes = np.zeros((plane, plane))
    from_modes = np.zeros((plane, plane))
    for slot, mode in enumerate(reps):
        theta = angle(mode)
        to_modes[:, slot] = np.cos(theta)
        to_modes[:, slots + slot] = -np.sin(theta)
        from_modes[slot] = 2.0 * np.cos(theta)
        from_modes[slots + slot] = -2.0 * np.sin(theta)
    for slot, (first, second) in enumerate(pairs, len(reps)):
        to_modes[:, slot] = from_modes[slot] = np.cos(angle(first))
        to_modes[:, slots + slot] = from_modes[slots + slot] = np.cos(angle(second))
    from_modes /= points * plane
    line = np.arange(points)
    theta = 2.0 * np.pi / points * (line[:, None] * line[None, :] % points)
    forward = np.block([[np.cos(theta), np.sin(theta)], [-np.sin(theta), np.cos(theta)]])
    forward = np.kron(forward, np.eye(sub))

    pick = np.zeros((2, plane, slots + lane), np.float32)

    def add(mode, column, weight):
        kb, kc = mode
        pick[0, kb * points + kc, column] += 0.5 * weight
        pick[1, -kb % points * points + -kc % points, column] += 0.5 * weight

    for slot, mode in enumerate(reps):
        add(mode, slot, 1.0)
    for slot, (first, second) in enumerate(pairs, len(reps)):
        add(first, slot, 0.5)
        add(second, slot, 0.5)
        add(first, slot + lane, 0.5)
        add(second, slot + lane, -0.5)
    return {
        "to_modes": split_table(to_modes),
        "from_modes": split_table(from_modes),
        "forward": split_table(forward),
        "backward": split_table(forward.T),
        "pick": jnp.asarray(pick.astype(jnp.bfloat16)),
    }


def split(values):
    high = values.astype(jnp.bfloat16)
    return high, (values - high.astype(jnp.float32)).astype(jnp.bfloat16)


def dot(a, b):
    return jnp.dot(a, b, preferred_element_type=jnp.float32)


def multiplier_kernel(gain, freq, pick, gain_out, freq_out):
    points = gain.shape[0]
    rows = jnp.concatenate([gain[...], freq[...]], axis=0)
    high, _ = split(rows)
    mid, low = split(rows - high.astype(jnp.float32))
    here, mirrored = (dot(low, pick[i]) + dot(mid, pick[i]) + dot(high, pick[i]) for i in range(2))
    for index, out in enumerate((gain_out, freq_out)):
        for a in range(points):
            at, turned = index * points + a, index * points + -a % points
            row = here[at : at + 1] + mirrored[turned : turned + 1]
            out[a * sub : (a + 1) * sub, :] = jnp.broadcast_to(row, (sub, row.shape[1]))


def multipliers(gain_spectrum, freq_spectrum, pick):
    points = gain_spectrum.shape[0]
    out = jax.ShapeDtypeStruct((points * sub, pick.shape[2]), jnp.float32)
    return pl.pallas_call(
        multiplier_kernel,
        in_specs=[local(pltpu.VMEM)] * 3,
        out_specs=[local(pltpu.VMEM)] * 2,
        out_shape=[out, out],
        compiler_params=pltpu.CompilerParams(vmem_limit_bytes=vmem_bytes),
        cost_estimate=pl.CostEstimate(flops=24 * points * pick.size, bytes_accessed=2 * pick.size, transcendentals=0),
    )(gain_spectrum.reshape(points, -1), freq_spectrum.reshape(points, -1), pick)


def partners(count):
    far = tuple(range(count // 2, count))
    return far, tuple(sorted(range(1, count // 2), key=lambda step: (-step.bit_length(), step)))


def swap(values, axis, step):
    return lax.ppermute(values, axis, [(i, i ^ step) for i in range(lax.axis_size(axis))])


def local(array):
    return pl.BlockSpec(memory_space=array)


def start_of(group, cells, low_groups, gap):
    return pl.multiple_of(group * cells + jnp.where(group < low_groups, 0, gap), sub)


def move_kernel(order, offset, low_groups, gap, points, has_halo, has_after, has_edges, me, particles, *rest):
    count = len(order)
    low, high = rest[:2] if has_halo else (None, None)
    outs = rest[2 * has_halo + has_after :][:count]
    edges = rest[2 * has_halo + has_after + count :][: 2 * has_edges]
    inside, made, rim, in_sems, out_sems = rest[-5:]
    cells, width = outs[0].shape
    total = particles.shape[0]
    planes = width // points**2
    span = inside.shape[1]
    at = me[0]

    def place(step):
        first = offset + start_of(at ^ step, cells, low_groups, gap)
        begin = pl.multiple_of(jnp.clip(first - sub, 0, total - span), sub)
        return first, begin

    def fetch(k, step):
        return pltpu.make_async_copy(particles.at[pl.ds(place(step)[1], span)], inside.at[k], in_sems.at[k])

    def store(k):
        return pltpu.make_async_copy(made.at[k], outs[k], out_sems.at[k])

    def edge_in(k):
        rows = pl.ds((total - sub) * k, sub)
        return pltpu.make_async_copy(particles.at[rows], rim.at[k], in_sems.at[count + k])

    def edge_out(k):
        return pltpu.make_async_copy(rim.at[k], edges[k], out_sems.at[count + k])

    for k, step in enumerate(order):
        fetch(k, step).start()
    for k in range(len(edges)):
        edge_in(k).start()
    for k, step in enumerate(order):
        fetch(k, step).wait()
        first, begin = place(step)
        skip = pl.multiple_of(first - begin, sub)
        ahead = pl.multiple_of(jnp.maximum(skip - sub, 0), sub)
        behind = pl.multiple_of(jnp.minimum(skip + cells, span - sub), sub)
        for plane in range(planes):
            columns = slice(plane * points**2, (plane + 1) * points**2)
            nu = courant * (2 * (at * planes + plane) + 1 - points).astype(jnp.float32) / points
            here = inside[k, pl.ds(skip, cells), columns]
            before = inside[k, pl.ds(ahead, sub), columns][sub - 1 :, :]
            after = inside[k, pl.ds(behind, sub), columns][:1, :]
            if has_halo:
                before = jnp.where(first == 0, low[sub - 1 :, columns], before)
                after = jnp.where(first + cells == total, high[:1, columns], after)
            row = lax.broadcasted_iota(jnp.int32, here.shape, 0)
            left = jnp.where(row == 0, before, pltpu.roll(here, 1, 0))
            right = jnp.where(row == cells - 1, after, pltpu.roll(here, cells - 1, 0))
            made[k, :, columns] = here - nu * jnp.where(nu > 0, here - left, right - here)
        store(k).start()
    for k in range(len(edges)):
        edge_in(k).wait()
        edge_out(k).start()
    for k in range(len(edges)):
        edge_out(k).wait()
    for k in range(count):
        store(k).wait()


def move(me, particles, order, cells, offset, low_groups, gap, points, halo=(), after=(), edges=False):
    total, width = particles.shape
    count = len(order)
    span = min(cells + 2 * sub, total)
    size = count * cells * width
    shape = jax.ShapeDtypeStruct((cells, width), jnp.float32)
    rim = jax.ShapeDtypeStruct((sub, width), jnp.float32)
    flags = (bool(halo), len(after), edges)
    return pl.pallas_call(
        functools.partial(move_kernel, order, offset, low_groups, gap, points, *flags),
        in_specs=[local(pltpu.SMEM), local(pltpu.HBM)]
        + [local(pltpu.VMEM)] * len(halo)
        + [local(pltpu.HBM)] * len(after),
        out_specs=[local(pltpu.HBM)] * (count + 2 * edges),
        out_shape=[shape] * count + [rim] * (2 * edges),
        scratch_shapes=[
            pltpu.VMEM((count, span, width), jnp.float32),
            pltpu.VMEM((count, cells, width), jnp.float32),
            pltpu.VMEM((2, sub, width), jnp.float32),
            pltpu.SemaphoreType.DMA((count + 2,)),
            pltpu.SemaphoreType.DMA((count + 2,)),
        ],
        compiler_params=pltpu.CompilerParams(vmem_limit_bytes=vmem_bytes),
        cost_estimate=pl.CostEstimate(flops=5 * size, bytes_accessed=10 * size, transcendentals=0),
    )(me, particles, *halo, *after)


def collide_kernel(steps, me, *rest):
    count = len(steps)
    xs, rest = rest[:count], rest[count:]
    to_high, to_low, from_high, from_low, ahead_high, ahead_low, back_high, back_low, gain, freq = rest[:10]
    outs, rest = rest[10 : 10 + count], rest[10 + count :]
    mass, wide_high, wide_low, mid, both_high, both_low, fields = rest
    cells, width = xs[0].shape
    plane = to_high.shape[0]
    slots = plane // 2
    planes = width // plane
    points = count * planes
    groups = cells // sub
    chunk = points * sub
    tile = min(256, plane)
    at = me[0]

    def pieces():
        for k, step in enumerate(steps):
            for group in range(groups):
                for j in range(planes):
                    start = (group * points + (at ^ step) * planes + j) * sub
                    here = (slice(group * sub, (group + 1) * sub), slice(j * plane, (j + 1) * plane))
                    yield k, group, here, pl.multiple_of(start, sub)

    for k, group, here, start in pieces():
        mid[pl.ds(start, sub), :] = xs[k][here]
    high, low = split(mid[...])
    wide_high[: groups * chunk, :] = high
    wide_low[: groups * chunk, :] = low

    @pl.loop(0, plane // tile)
    def _(at):
        columns = pl.ds(pl.multiple_of(at * tile, tile), tile)
        table = to_high[:, columns]
        mid[:, columns] = (
            dot(wide_low[: groups * chunk, :], table)
            + dot(wide_high[: groups * chunk, :], to_low[:, columns])
            + dot(wide_high[: groups * chunk, :], table)
        )

    @pl.loop(0, groups)
    def _(group):
        rows = pl.ds(pl.multiple_of(group * chunk, chunk), chunk)
        spectrum = jnp.concatenate([mid[rows, :slots], mid[rows, slots:]], axis=0)
        high, low = split(spectrum)
        waves = dot(ahead_high[...], low) + dot(ahead_low[...], high) + dot(ahead_high[...], high)
        real, imag = waves[:chunk], waves[chunk:]

        def mirror(values):
            tail = values[:, slots - lane :]
            turned = [tail[-a % points * sub : (-a % points + 1) * sub] for a in range(points)]
            return jnp.concatenate(turned, axis=0)

        real_tail, imag_tail = mirror(real), mirror(imag)
        for index, table in enumerate((gain, freq)):
            pad = jnp.zeros((chunk, slots - lane), jnp.float32)
            extra = table[:, slots:]
            upper = real * table[:, :slots] + jnp.concatenate([pad, real_tail * extra], axis=1)
            lower = imag * table[:, :slots] - jnp.concatenate([pad, imag_tail * extra], axis=1)
            for start, values in ((0, upper), (chunk, lower)):
                high, low = split(values)
                both_high[start : start + chunk, index * slots : (index + 1) * slots] = high
                both_low[start : start + chunk, index * slots : (index + 1) * slots] = low
        for index in range(2):
            columns = slice(index * slots, (index + 1) * slots)
            lines = (
                dot(back_high[...], both_low[:, columns])
                + dot(back_low[...], both_high[:, columns])
                + dot(back_high[...], both_high[:, columns])
            )
            high, low = split(jnp.concatenate([lines[:chunk], lines[chunk:]], axis=1))
            at = pl.ds(pl.multiple_of((index * groups + group) * chunk, chunk), chunk)
            wide_high[at, :] = high
            wide_low[at, :] = low

    @pl.loop(0, plane // tile)
    def _(at):
        columns = pl.ds(pl.multiple_of(at * tile, tile), tile)
        table = from_high[:, columns]
        fields[:, columns] = (
            dot(wide_low[...], table) + dot(wide_high[...], from_low[:, columns]) + dot(wide_high[...], table)
        )

    totals = [jnp.zeros((sub, plane), jnp.float32)] * groups
    for k, group, here, start in pieces():
        cube = xs[k][here]
        gained = fields[pl.ds(start, sub), :]
        lost = fields[pl.ds(pl.multiple_of(groups * chunk + start, sub), sub), :]
        post = cube + collide_rate * (gained - cube * lost)
        outs[k][here] = post
        totals[group] = totals[group] + post
    for group, total in enumerate(totals):
        lanes = total[:, :lane]
        for column in range(lane, plane, lane):
            lanes = lanes + total[:, column : column + lane]
        mass[group * sub : (group + 1) * sub, :] = lanes


def collide(me, cubes, steps, tables, gain, freq):
    cells, width = cubes[0].shape
    count = len(cubes)
    plane = tables["to_modes"][0].shape[0]
    points = count * width // plane
    step = math.gcd(cells, 2 * sub)
    chunk = step * points
    operands = [*tables["to_modes"], *tables["from_modes"], *tables["forward"], *tables["backward"], gain, freq]
    bf16, f32 = jnp.bfloat16, jnp.float32
    block = pl.BlockSpec((step, width), lambda i: (i, 0))
    multiply_adds = 3 * cells * points * (3 * plane * plane + 6 * points * sub * plane)
    *posts, mass = pl.pallas_call(
        functools.partial(collide_kernel, steps),
        grid=(cells // step,),
        in_specs=[local(pltpu.SMEM)] + [block] * count + [local(pltpu.VMEM)] * len(operands),
        out_specs=[block] * count + [pl.BlockSpec((step, lane), lambda i: (i, 0))],
        out_shape=[jax.ShapeDtypeStruct((cells, width), f32)] * count + [jax.ShapeDtypeStruct((cells, lane), f32)],
        scratch_shapes=[
            pltpu.VMEM((2 * chunk, plane), bf16),
            pltpu.VMEM((2 * chunk, plane), bf16),
            pltpu.VMEM((chunk, plane), f32),
            pltpu.VMEM((2 * points * sub, plane), bf16),
            pltpu.VMEM((2 * points * sub, plane), bf16),
            pltpu.VMEM((2 * chunk, plane), f32),
        ],
        compiler_params=pltpu.CompilerParams(vmem_limit_bytes=vmem_bytes),
        cost_estimate=pl.CostEstimate(
            flops=3 * multiply_adds, bytes_accessed=8 * count * cells * width, transcendentals=0
        ),
    )(me, *cubes, *operands)
    return posts, mass


def mass_kernel(count, *refs):
    parts, out = refs[:count], refs[-1]
    total = jnp.zeros(out.shape, jnp.float32)
    for mass, member in zip(parts[::2], parts[1::2]):
        cell = jnp.sum(mass[...], axis=1, keepdims=True)
        total = total + jnp.sum(member[...] * cell, axis=0, keepdims=True)
    out[...] = total


def panel_mass(pairs, after):
    flat = [array for pair in pairs for array in pair]
    return pl.pallas_call(
        functools.partial(mass_kernel, len(flat)),
        in_specs=[local(pltpu.VMEM)] * len(flat) + [local(pl.ANY)] * len(after),
        out_specs=local(pltpu.VMEM),
        out_shape=jax.ShapeDtypeStruct((1, flat[1].shape[1]), jnp.float32),
    )(*flat, *after)


def settle_kernel(groups, me, member, emit, *rest):
    count = len(groups)
    posts = rest[:count]
    out, held, emission, in_sems, out_sems = rest[-5:]
    cells = held.shape[1]
    at = me[0]

    def fetch(k):
        return pltpu.make_async_copy(posts[k], held.at[k], in_sems.at[k])

    def store(k):
        step, (offset, low_groups, gap) = groups[k]
        first = offset + start_of(at ^ step, cells, low_groups, gap)
        return pltpu.make_async_copy(held.at[k], out.at[pl.ds(first, cells)], out_sems.at[k])

    for k in range(count):
        fetch(k).start()
    chosen = member[...]
    share = accommodation * jnp.sum(chosen, axis=1, keepdims=True)
    emission[...] = dot(jnp.concatenate([chosen, chosen], axis=1).astype(jnp.bfloat16), emit[...])
    for k in range(count):
        fetch(k).wait()
        rows = slice(k * cells, (k + 1) * cells)
        post = held[k]
        held[k] = post + (accommodation * emission[rows, :] - share[rows] * post)
        store(k).start()
    for k in range(count):
        store(k).wait()


def settle(me, posts, groups, member, emit, earlier, shape):
    cells, width = posts[0].shape
    count = len(posts)
    size = count * cells * width
    operands = [me, member, emit, *posts]
    in_specs = [local(pltpu.SMEM), local(pltpu.VMEM), local(pltpu.VMEM)] + [local(pl.ANY)] * count
    aliases = {}
    if earlier is not None:
        aliases = {len(operands): 0}
        operands.append(earlier)
        in_specs.append(local(pltpu.HBM))
    return pl.pallas_call(
        functools.partial(settle_kernel, groups),
        in_specs=in_specs,
        out_specs=local(pltpu.HBM),
        out_shape=jax.ShapeDtypeStruct(shape, jnp.float32),
        scratch_shapes=[
            pltpu.VMEM((count, cells, width), jnp.float32),
            pltpu.VMEM((count * cells, width), jnp.float32),
            pltpu.SemaphoreType.DMA((count,)),
            pltpu.SemaphoreType.DMA((count,)),
        ],
        input_output_aliases=aliases,
        compiler_params=pltpu.CompilerParams(vmem_limit_bytes=8 * size + 6 * 2**20),
        cost_estimate=pl.CostEstimate(
            flops=4 * member.shape[1] * size, bytes_accessed=8 * size, transcendentals=0
        ),
    )(*operands)


def on_device(particles, gain_spectrum, freq_spectrum, panel_temp, wall_cells):
    cell_dev, vel_dev = particles.shape
    points = gain_spectrum.shape[0]
    plane_size = points * points
    planes = vel_dev // plane_size
    vel_count = lax.axis_size("vel")
    vel_at = lax.axis_index("vel")
    space_at = lax.axis_index("space")
    space_count = lax.axis_size("space")
    me = vel_at.astype(jnp.int32)[None]
    tables = dft_tables(points)
    panels, per_panel = wall_cells.shape

    quarter, half = cell_dev // 4, cell_dev // 2
    cells = half // vel_count
    inner, outer = (quarter, vel_count, 0), (0, vel_count // 2, half)
    far, near = partners(vel_count)
    steps = (*far, *near, 0)
    urgent, ready = far[:1], (*far, *near[:1])

    def send(arrays):
        return {step: swap(array, "vel", step) if step else array for step, array in arrays.items()}

    def rest(done):
        return tuple(step for step in steps if step not in done)

    early = move(me, particles, urgent, cells, *inner, points)
    *late, first_rows, last_rows = move(
        me, particles, rest(urgent), cells, *inner, points, after=early[:1], edges=True
    )
    inner_moved = dict(zip((*urgent, *rest(urgent)), (*early, *late)))
    inner_cubes = send({step: inner_moved[step] for step in far})
    behind, ahead = near, far[:1]
    tied = lax.optimization_barrier(tuple(inner_moved[step] for step in behind) + tuple(inner_cubes[step] for step in ahead))
    inner_moved.update(zip(behind, tied))
    inner_cubes.update(zip(ahead, tied[len(behind) :]))
    inner_cubes.update(send({step: inner_moved[step] for step in (*near, 0)}))
    space_pairs = [(i, i + 1) for i in range(space_count - 1)]
    low = lax.ppermute(last_rows, "space", space_pairs)
    high = lax.ppermute(first_rows, "space", [(target, source) for source, target in space_pairs])
    outer_early = move(me, particles, ready, cells, *outer, points, halo=(low, high))
    gain, freq = multipliers(gain_spectrum, freq_spectrum, tables["pick"])

    def collided(cubes):
        posts, mass = collide(me, [cubes[step] for step in steps], steps, tables, gain, freq)
        return dict(zip(steps, posts)), mass

    inner_posts, inner_mass = collided(inner_cubes)
    outer_late = move(
        me, particles, rest(ready), cells, *outer, points, halo=(low, high), after=(inner_mass,)
    )
    outer_cubes = send(dict(zip((*ready, *rest(ready)), (*outer_early, *outer_late))))
    outer_posts, outer_mass = collided(outer_cubes)

    def cells_of(plan, group):
        offset, low_groups, gap = plan
        first = offset + group * cells + jnp.where(group < low_groups, 0, gap)
        return space_at * cell_dev + first + jnp.arange(cells, dtype=jnp.int32)

    def membership(cell_ids):
        hit = wall_cells.reshape(1, panels, per_panel) == cell_ids[:, None, None]
        return jnp.any(hit, axis=2).astype(jnp.float32)

    held = near
    *tied, outer_mass = lax.optimization_barrier((*(inner_posts[step] for step in held), outer_mass))
    inner_back = send({**inner_posts, **dict(zip(held, tied))})
    outer_back = send(outer_posts)
    pairs = [
        (mass, membership(cells_of(plan, vel_at))) for mass, plan in ((inner_mass, inner), (outer_mass, outer))
    ]
    wall_mass = lax.psum(panel_mass(pairs, [inner_back[step] for step in (*far, *near)]), "space")
    step = 1
    while step < vel_count:
        wall_mass = wall_mass + swap(wall_mass, "vel", step)
        step *= 2

    def speed(index):
        return top_speed * (2 * index + 1 - points).astype(jnp.float32) / points

    line = jnp.arange(points, dtype=jnp.int32)
    line_weight = jnp.exp(-(speed(line) ** 2)[None, :] / (2.0 * panel_temp[:, None]))
    normal_sum = jnp.sum(line_weight, axis=1) ** 3
    columns = jnp.arange(vel_dev, dtype=jnp.int32)
    plane_index = vel_at * planes + columns // plane_size
    speed_sq = speed(plane_index) ** 2 + speed(columns // points % points) ** 2 + speed(columns % points) ** 2
    profile = jnp.exp(-speed_sq[None, :] / (2.0 * panel_temp[:, None]))
    maxwellian = profile / normal_sum[:, None]
    emission = (wall_mass.reshape(panels, 1) / per_panel) * maxwellian
    emit_high = lax.reduce_precision(emission, exponent_bits=8, mantissa_bits=7)
    emit = jnp.concatenate([emit_high, emission - emit_high], axis=0).astype(jnp.bfloat16)

    def wall(arrived, earlier):
        groups, posts = zip(*arrived)
        ids = jnp.concatenate([cells_of(plan, vel_at ^ step) for step, plan in groups])
        return settle(me, posts, groups, membership(ids), emit, earlier, particles.shape)

    final = (*near[:2], far[2], *near[2:], *far[3:])
    first = [((step, inner), inner_back[step]) for step in steps]
    first += [((step, outer), outer_back[step]) for step in rest(final)]
    return wall([((step, outer), outer_back[step]) for step in final], wall(first, None))


def solution(mesh):
    in_specs = (P("space", "vel"), P(), P(), P(), P())
    out_specs = P("space", "vel")
    return jax.shard_map(on_device, mesh=mesh, in_specs=in_specs, out_specs=out_specs, check_vma=False)
```

```python
import functools
import math

import jax
import jax.numpy as jnp
import numpy as np
from jax import lax
from jax.experimental import pallas as pl
from jax.experimental.pallas import tpu as pltpu
from jax.sharding import PartitionSpec as P

courant = 0.9
top_speed = 3.0
collide_rate = 0.5
accommodation = 0.8
highest = lax.Precision.HIGHEST
sub = 8
lane = 128
vmem_bytes = 56 * 2**20


def split_table(table):
    high = table.astype(np.float32).astype(jnp.bfloat16)
    low = (table - high.astype(np.float64)).astype(np.float32).astype(jnp.bfloat16)
    return jnp.asarray(high), jnp.asarray(low)


def dft_tables(points):
    half = points // 2
    plane = points * points
    self_modes = [(0, 0), (0, half), (half, 0), (half, half)]
    reps = [(kb, kc) for kb in range(points) for kc in range(1, half)]
    reps += [(kb, 0) for kb in range(1, half)] + [(kb, half) for kb in range(1, half)]
    pairs = [(self_modes[0], self_modes[1]), (self_modes[2], self_modes[3])]
    slots = len(reps) + len(pairs)
    outer, inner = np.divmod(np.arange(plane), points)

    def angle(mode):
        return 2.0 * np.pi / points * ((outer * mode[0] + inner * mode[1]) % points)

    to_modes = np.zeros((plane, plane))
    from_modes = np.zeros((plane, plane))
    for slot, mode in enumerate(reps):
        theta = angle(mode)
        to_modes[:, slot] = np.cos(theta)
        to_modes[:, slots + slot] = -np.sin(theta)
        from_modes[slot] = 2.0 * np.cos(theta)
        from_modes[slots + slot] = -2.0 * np.sin(theta)
    for slot, (first, second) in enumerate(pairs, len(reps)):
        to_modes[:, slot] = from_modes[slot] = np.cos(angle(first))
        to_modes[:, slots + slot] = from_modes[slots + slot] = np.cos(angle(second))
    from_modes /= points * plane
    line = np.arange(points)
    theta = 2.0 * np.pi / points * (line[:, None] * line[None, :] % points)
    forward = np.block([[np.cos(theta), np.sin(theta)], [-np.sin(theta), np.cos(theta)]])
    forward = np.kron(forward, np.eye(sub))

    pick = np.zeros((2, plane, slots + lane), np.float32)

    def add(mode, column, weight):
        kb, kc = mode
        pick[0, kb * points + kc, column] += 0.5 * weight
        pick[1, -kb % points * points + -kc % points, column] += 0.5 * weight

    for slot, mode in enumerate(reps):
        add(mode, slot, 1.0)
    for slot, (first, second) in enumerate(pairs, len(reps)):
        add(first, slot, 0.5)
        add(second, slot, 0.5)
        add(first, slot + lane, 0.5)
        add(second, slot + lane, -0.5)
    return {
        "to_modes": split_table(to_modes),
        "from_modes": split_table(from_modes),
        "forward": split_table(forward),
        "backward": split_table(forward.T),
        "pick": jnp.asarray(pick.astype(jnp.bfloat16)),
    }


def split(values):
    high = values.astype(jnp.bfloat16)
    return high, (values - high.astype(jnp.float32)).astype(jnp.bfloat16)


def dot(a, b):
    return jnp.dot(a, b, preferred_element_type=jnp.float32)


def multiplier_kernel(gain, freq, pick, gain_out, freq_out):
    points = gain.shape[0]
    rows = jnp.concatenate([gain[...], freq[...]], axis=0)
    high, _ = split(rows)
    mid, low = split(rows - high.astype(jnp.float32))
    here, mirrored = (dot(low, pick[i]) + dot(mid, pick[i]) + dot(high, pick[i]) for i in range(2))
    for index, out in enumerate((gain_out, freq_out)):
        for a in range(points):
            at, turned = index * points + a, index * points + -a % points
            row = here[at : at + 1] + mirrored[turned : turned + 1]
            out[a * sub : (a + 1) * sub, :] = jnp.broadcast_to(row, (sub, row.shape[1]))


def multipliers(gain_spectrum, freq_spectrum, pick):
    points = gain_spectrum.shape[0]
    out = jax.ShapeDtypeStruct((points * sub, pick.shape[2]), jnp.float32)
    return pl.pallas_call(
        multiplier_kernel,
        in_specs=[local(pltpu.VMEM)] * 3,
        out_specs=[local(pltpu.VMEM)] * 2,
        out_shape=[out, out],
        compiler_params=pltpu.CompilerParams(vmem_limit_bytes=vmem_bytes),
        cost_estimate=pl.CostEstimate(flops=24 * points * pick.size, bytes_accessed=2 * pick.size, transcendentals=0),
    )(gain_spectrum.reshape(points, -1), freq_spectrum.reshape(points, -1), pick)


def partners(count):
    far = tuple(range(count // 2, count))
    return far, tuple(sorted(range(1, count // 2), key=lambda step: (-step.bit_length(), step)))


def swap(values, axis, step):
    return lax.ppermute(values, axis, [(i, i ^ step) for i in range(lax.axis_size(axis))])


def local(array):
    return pl.BlockSpec(memory_space=array)


def start_of(group, cells, low_groups, gap):
    return pl.multiple_of(group * cells + jnp.where(group < low_groups, 0, gap), sub)


def move_kernel(order, offset, low_groups, gap, points, has_halo, has_after, has_edges, me, particles, *rest):
    count = len(order)
    low, high = rest[:2] if has_halo else (None, None)
    outs = rest[2 * has_halo + has_after :][:count]
    edges = rest[2 * has_halo + has_after + count :][: 2 * has_edges]
    inside, made, rim, in_sems, out_sems = rest[-5:]
    cells, width = outs[0].shape
    total = particles.shape[0]
    planes = width // points**2
    span = inside.shape[1]
    at = me[0]

    def place(step):
        first = offset + start_of(at ^ step, cells, low_groups, gap)
        begin = pl.multiple_of(jnp.clip(first - sub, 0, total - span), sub)
        return first, begin

    def fetch(k, step):
        return pltpu.make_async_copy(particles.at[pl.ds(place(step)[1], span)], inside.at[k], in_sems.at[k])

    def store(k):
        return pltpu.make_async_copy(made.at[k], outs[k], out_sems.at[k])

    def edge_in(k):
        rows = pl.ds((total - sub) * k, sub)
        return pltpu.make_async_copy(particles.at[rows], rim.at[k], in_sems.at[count + k])

    def edge_out(k):
        return pltpu.make_async_copy(rim.at[k], edges[k], out_sems.at[count + k])

    for k, step in enumerate(order):
        fetch(k, step).start()
    for k in range(len(edges)):
        edge_in(k).start()
    for k, step in enumerate(order):
        fetch(k, step).wait()
        first, begin = place(step)
        skip = pl.multiple_of(first - begin, sub)
        ahead = pl.multiple_of(jnp.maximum(skip - sub, 0), sub)
        behind = pl.multiple_of(jnp.minimum(skip + cells, span - sub), sub)
        for plane in range(planes):
            columns = slice(plane * points**2, (plane + 1) * points**2)
            nu = courant * (2 * (at * planes + plane) + 1 - points).astype(jnp.float32) / points
            here = inside[k, pl.ds(skip, cells), columns]
            before = inside[k, pl.ds(ahead, sub), columns][sub - 1 :, :]
            after = inside[k, pl.ds(behind, sub), columns][:1, :]
            if has_halo:
                before = jnp.where(first == 0, low[sub - 1 :, columns], before)
                after = jnp.where(first + cells == total, high[:1, columns], after)
            row = lax.broadcasted_iota(jnp.int32, here.shape, 0)
            left = jnp.where(row == 0, before, pltpu.roll(here, 1, 0))
            right = jnp.where(row == cells - 1, after, pltpu.roll(here, cells - 1, 0))
            made[k, :, columns] = here - nu * jnp.where(nu > 0, here - left, right - here)
        store(k).start()
    for k in range(len(edges)):
        edge_in(k).wait()
        edge_out(k).start()
    for k in range(len(edges)):
        edge_out(k).wait()
    for k in range(count):
        store(k).wait()


def move(me, particles, order, cells, offset, low_groups, gap, points, halo=(), after=(), edges=False):
    total, width = particles.shape
    count = len(order)
    span = min(cells + 2 * sub, total)
    size = count * cells * width
    shape = jax.ShapeDtypeStruct((cells, width), jnp.float32)
    rim = jax.ShapeDtypeStruct((sub, width), jnp.float32)
    flags = (bool(halo), len(after), edges)
    return pl.pallas_call(
        functools.partial(move_kernel, order, offset, low_groups, gap, points, *flags),
        in_specs=[local(pltpu.SMEM), local(pltpu.HBM)]
        + [local(pltpu.VMEM)] * len(halo)
        + [local(pltpu.HBM)] * len(after),
        out_specs=[local(pl.ANY)] * (count + 2 * edges),
        out_shape=[shape] * count + [rim] * (2 * edges),
        scratch_shapes=[
            pltpu.VMEM((count, span, width), jnp.float32),
            pltpu.VMEM((count, cells, width), jnp.float32),
            pltpu.VMEM((2, sub, width), jnp.float32),
            pltpu.SemaphoreType.DMA((count + 2,)),
            pltpu.SemaphoreType.DMA((count + 2,)),
        ],
        compiler_params=pltpu.CompilerParams(vmem_limit_bytes=4 * count * (span + cells) * width + 6 * 2**20),
        cost_estimate=pl.CostEstimate(flops=5 * size, bytes_accessed=10 * size, transcendentals=0),
    )(me, particles, *halo, *after)


def collide_kernel(steps, me, *rest):
    count = len(steps)
    xs, rest = rest[:count], rest[count:]
    to_high, to_low, from_high, from_low, ahead_high, ahead_low, back_high, back_low, gain, freq = rest[:10]
    outs, rest = rest[10 : 10 + count], rest[10 + count :]
    mass, wide_high, wide_low, mid, both_high, both_low, fields = rest
    cells, width = xs[0].shape
    plane = to_high.shape[0]
    slots = plane // 2
    planes = width // plane
    points = count * planes
    groups = cells // sub
    chunk = points * sub
    tile = min(256, plane)
    at = me[0]

    def pieces():
        for k, step in enumerate(steps):
            for group in range(groups):
                for j in range(planes):
                    start = (group * points + (at ^ step) * planes + j) * sub
                    here = (slice(group * sub, (group + 1) * sub), slice(j * plane, (j + 1) * plane))
                    yield k, group, here, pl.multiple_of(start, sub)

    for k, group, here, start in pieces():
        mid[pl.ds(start, sub), :] = xs[k][here]
    high, low = split(mid[...])
    wide_high[: groups * chunk, :] = high
    wide_low[: groups * chunk, :] = low

    @pl.loop(0, plane // tile)
    def _(at):
        columns = pl.ds(pl.multiple_of(at * tile, tile), tile)
        table = to_high[:, columns]
        mid[:, columns] = (
            dot(wide_low[: groups * chunk, :], table)
            + dot(wide_high[: groups * chunk, :], to_low[:, columns])
            + dot(wide_high[: groups * chunk, :], table)
        )

    @pl.loop(0, groups)
    def _(group):
        rows = pl.ds(pl.multiple_of(group * chunk, chunk), chunk)
        spectrum = jnp.concatenate([mid[rows, :slots], mid[rows, slots:]], axis=0)
        high, low = split(spectrum)
        waves = dot(ahead_high[...], low) + dot(ahead_low[...], high) + dot(ahead_high[...], high)
        real, imag = waves[:chunk], waves[chunk:]

        def mirror(values):
            tail = values[:, slots - lane :]
            turned = [tail[-a % points * sub : (-a % points + 1) * sub] for a in range(points)]
            return jnp.concatenate(turned, axis=0)

        real_tail, imag_tail = mirror(real), mirror(imag)
        for index, table in enumerate((gain, freq)):
            pad = jnp.zeros((chunk, slots - lane), jnp.float32)
            extra = table[:, slots:]
            upper = real * table[:, :slots] + jnp.concatenate([pad, real_tail * extra], axis=1)
            lower = imag * table[:, :slots] - jnp.concatenate([pad, imag_tail * extra], axis=1)
            for start, values in ((0, upper), (chunk, lower)):
                high, low = split(values)
                both_high[start : start + chunk, index * slots : (index + 1) * slots] = high
                both_low[start : start + chunk, index * slots : (index + 1) * slots] = low
        for index in range(2):
            columns = slice(index * slots, (index + 1) * slots)
            lines = (
                dot(back_high[...], both_low[:, columns])
                + dot(back_low[...], both_high[:, columns])
                + dot(back_high[...], both_high[:, columns])
            )
            high, low = split(jnp.concatenate([lines[:chunk], lines[chunk:]], axis=1))
            at = pl.ds(pl.multiple_of((index * groups + group) * chunk, chunk), chunk)
            wide_high[at, :] = high
            wide_low[at, :] = low

    @pl.loop(0, plane // tile)
    def _(at):
        columns = pl.ds(pl.multiple_of(at * tile, tile), tile)
        table = from_high[:, columns]
        fields[:, columns] = (
            dot(wide_low[...], table) + dot(wide_high[...], from_low[:, columns]) + dot(wide_high[...], table)
        )

    totals = [jnp.zeros((sub, plane), jnp.float32)] * groups
    for k, group, here, start in pieces():
        cube = xs[k][here]
        gained = fields[pl.ds(start, sub), :]
        lost = fields[pl.ds(pl.multiple_of(groups * chunk + start, sub), sub), :]
        post = cube + collide_rate * (gained - cube * lost)
        outs[k][here] = post
        totals[group] = totals[group] + post
    for group, total in enumerate(totals):
        lanes = total[:, :lane]
        for column in range(lane, plane, lane):
            lanes = lanes + total[:, column : column + lane]
        mass[group * sub : (group + 1) * sub, :] = lanes


def collide(me, cubes, steps, tables, gain, freq):
    cells, width = cubes[0].shape
    count = len(cubes)
    plane = tables["to_modes"][0].shape[0]
    points = count * width // plane
    step = math.gcd(cells, 2 * sub)
    chunk = step * points
    operands = [*tables["to_modes"], *tables["from_modes"], *tables["forward"], *tables["backward"], gain, freq]
    bf16, f32 = jnp.bfloat16, jnp.float32
    block = pl.BlockSpec((step, width), lambda i: (i, 0))
    multiply_adds = 3 * cells * points * (3 * plane * plane + 6 * points * sub * plane)
    *posts, mass = pl.pallas_call(
        functools.partial(collide_kernel, steps),
        grid=(cells // step,),
        in_specs=[local(pltpu.SMEM)] + [block] * count + [local(pltpu.VMEM)] * len(operands),
        out_specs=[block] * count + [pl.BlockSpec((step, lane), lambda i: (i, 0))],
        out_shape=[jax.ShapeDtypeStruct((cells, width), f32)] * count + [jax.ShapeDtypeStruct((cells, lane), f32)],
        scratch_shapes=[
            pltpu.VMEM((2 * chunk, plane), bf16),
            pltpu.VMEM((2 * chunk, plane), bf16),
            pltpu.VMEM((chunk, plane), f32),
            pltpu.VMEM((2 * points * sub, plane), bf16),
            pltpu.VMEM((2 * points * sub, plane), bf16),
            pltpu.VMEM((2 * chunk, plane), f32),
        ],
        compiler_params=pltpu.CompilerParams(vmem_limit_bytes=vmem_bytes),
        cost_estimate=pl.CostEstimate(
            flops=3 * multiply_adds, bytes_accessed=8 * count * cells * width, transcendentals=0
        ),
    )(me, *cubes, *operands)
    return posts, mass


def mass_kernel(count, *refs):
    parts, out = refs[:count], refs[-1]
    total = jnp.zeros(out.shape, jnp.float32)
    for mass, member in zip(parts[::2], parts[1::2]):
        cell = jnp.sum(mass[...], axis=1, keepdims=True)
        total = total + jnp.sum(member[...] * cell, axis=0, keepdims=True)
    out[...] = total


def panel_mass(pairs, after):
    flat = [array for pair in pairs for array in pair]
    return pl.pallas_call(
        functools.partial(mass_kernel, len(flat)),
        in_specs=[local(pltpu.VMEM)] * len(flat) + [local(pl.ANY)] * len(after),
        out_specs=local(pltpu.VMEM),
        out_shape=jax.ShapeDtypeStruct((1, flat[1].shape[1]), jnp.float32),
    )(*flat, *after)


def settle_kernel(groups, me, member, emit, *rest):
    count = len(groups)
    posts = rest[:count]
    out, held, emission, in_sems, out_sems = rest[-5:]
    cells = held.shape[1]
    at = me[0]

    def fetch(k):
        return pltpu.make_async_copy(posts[k], held.at[k], in_sems.at[k])

    def store(k):
        step, (offset, low_groups, gap) = groups[k]
        first = offset + start_of(at ^ step, cells, low_groups, gap)
        return pltpu.make_async_copy(held.at[k], out.at[pl.ds(first, cells)], out_sems.at[k])

    for k in range(count):
        fetch(k).start()
    chosen = member[...]
    share = accommodation * jnp.sum(chosen, axis=1, keepdims=True)
    emission[...] = dot(jnp.concatenate([chosen, chosen], axis=1).astype(jnp.bfloat16), emit[...])
    for k in range(count):
        fetch(k).wait()
        rows = slice(k * cells, (k + 1) * cells)
        post = held[k]
        held[k] = post + (accommodation * emission[rows, :] - share[rows] * post)
        store(k).start()
    for k in range(count):
        store(k).wait()


def settle(me, posts, groups, member, emit, earlier, shape):
    cells, width = posts[0].shape
    count = len(posts)
    size = count * cells * width
    operands = [me, member, emit, *posts]
    in_specs = [local(pltpu.SMEM), local(pltpu.VMEM), local(pltpu.VMEM)] + [local(pl.ANY)] * count
    aliases = {}
    if earlier is not None:
        aliases = {len(operands): 0}
        operands.append(earlier)
        in_specs.append(local(pltpu.HBM))
    return pl.pallas_call(
        functools.partial(settle_kernel, groups),
        in_specs=in_specs,
        out_specs=local(pltpu.HBM),
        out_shape=jax.ShapeDtypeStruct(shape, jnp.float32),
        scratch_shapes=[
            pltpu.VMEM((count, cells, width), jnp.float32),
            pltpu.VMEM((count * cells, width), jnp.float32),
            pltpu.SemaphoreType.DMA((count,)),
            pltpu.SemaphoreType.DMA((count,)),
        ],
        input_output_aliases=aliases,
        compiler_params=pltpu.CompilerParams(vmem_limit_bytes=8 * size + 6 * 2**20),
        cost_estimate=pl.CostEstimate(
            flops=4 * member.shape[1] * size, bytes_accessed=8 * size, transcendentals=0
        ),
    )(*operands)


def on_device(particles, gain_spectrum, freq_spectrum, panel_temp, wall_cells):
    cell_dev, vel_dev = particles.shape
    points = gain_spectrum.shape[0]
    plane_size = points * points
    planes = vel_dev // plane_size
    vel_count = lax.axis_size("vel")
    vel_at = lax.axis_index("vel")
    space_at = lax.axis_index("space")
    space_count = lax.axis_size("space")
    me = vel_at.astype(jnp.int32)[None]
    tables = dft_tables(points)
    panels, per_panel = wall_cells.shape

    quarter, half = cell_dev // 4, cell_dev // 2
    cells = half // vel_count
    inner, outer = (quarter, vel_count, 0), (0, vel_count // 2, half)
    far, near = partners(vel_count)
    steps = (*far, *near, 0)
    urgent, ready = far[:1], (*far, *near[:2])

    def send(arrays):
        return {step: swap(array, "vel", step) if step else array for step, array in arrays.items()}

    def rest(done):
        return tuple(step for step in steps if step not in done)

    early = move(me, particles, urgent, cells, *inner, points)
    *late, first_rows, last_rows = move(
        me, particles, rest(urgent), cells, *inner, points, after=early[:1], edges=True
    )
    inner_moved = dict(zip((*urgent, *rest(urgent)), (*early, *late)))
    inner_cubes = send({step: inner_moved[step] for step in far})
    behind, ahead = near, far[:1]
    tied = lax.optimization_barrier(tuple(inner_moved[step] for step in behind) + tuple(inner_cubes[step] for step in ahead))
    inner_moved.update(zip(behind, tied))
    inner_cubes.update(zip(ahead, tied[len(behind) :]))
    inner_cubes.update(send({step: inner_moved[step] for step in (*near, 0)}))
    space_pairs = [(i, i + 1) for i in range(space_count - 1)]
    low = lax.ppermute(last_rows, "space", space_pairs)
    high = lax.ppermute(first_rows, "space", [(target, source) for source, target in space_pairs])
    outer_early = move(me, particles, ready, cells, *outer, points, halo=(low, high))
    gain, freq = multipliers(gain_spectrum, freq_spectrum, tables["pick"])

    def collided(cubes):
        posts, mass = collide(me, [cubes[step] for step in steps], steps, tables, gain, freq)
        return dict(zip(steps, posts)), mass

    inner_posts, inner_mass = collided(inner_cubes)
    outer_late = move(
        me, particles, rest(ready), cells, *outer, points, halo=(low, high), after=(inner_mass,)
    )
    outer_cubes = send(dict(zip((*ready, *rest(ready)), (*outer_early, *outer_late))))
    outer_posts, outer_mass = collided(outer_cubes)

    def cells_of(plan, group):
        offset, low_groups, gap = plan
        first = offset + group * cells + jnp.where(group < low_groups, 0, gap)
        return space_at * cell_dev + first + jnp.arange(cells, dtype=jnp.int32)

    def membership(cell_ids):
        hit = wall_cells.reshape(1, panels, per_panel) == cell_ids[:, None, None]
        return jnp.any(hit, axis=2).astype(jnp.float32)

    held = near
    *tied, outer_mass = lax.optimization_barrier((*(inner_posts[step] for step in held), outer_mass))
    inner_back = send({**inner_posts, **dict(zip(held, tied))})
    outer_back = send(outer_posts)
    pairs = [
        (mass, membership(cells_of(plan, vel_at))) for mass, plan in ((inner_mass, inner), (outer_mass, outer))
    ]
    wall_mass = lax.psum(panel_mass(pairs, [inner_back[step] for step in (*far, *near)]), "space")
    step = 1
    while step < vel_count:
        wall_mass = wall_mass + swap(wall_mass, "vel", step)
        step *= 2

    def speed(index):
        return top_speed * (2 * index + 1 - points).astype(jnp.float32) / points

    line = jnp.arange(points, dtype=jnp.int32)
    line_weight = jnp.exp(-(speed(line) ** 2)[None, :] / (2.0 * panel_temp[:, None]))
    normal_sum = jnp.sum(line_weight, axis=1) ** 3
    columns = jnp.arange(vel_dev, dtype=jnp.int32)
    plane_index = vel_at * planes + columns // plane_size
    speed_sq = speed(plane_index) ** 2 + speed(columns // points % points) ** 2 + speed(columns % points) ** 2
    profile = jnp.exp(-speed_sq[None, :] / (2.0 * panel_temp[:, None]))
    maxwellian = profile / normal_sum[:, None]
    emission = (wall_mass.reshape(panels, 1) / per_panel) * maxwellian
    emit_high = lax.reduce_precision(emission, exponent_bits=8, mantissa_bits=7)
    emit = jnp.concatenate([emit_high, emission - emit_high], axis=0).astype(jnp.bfloat16)

    def wall(arrived, earlier):
        groups, posts = zip(*arrived)
        ids = jnp.concatenate([cells_of(plan, vel_at ^ step) for step, plan in groups])
        return settle(me, posts, groups, membership(ids), emit, earlier, particles.shape)

    final = (*near[:2], far[2], *near[2:], *far[3:])
    first = [((step, inner), inner_back[step]) for step in steps]
    first += [((step, outer), outer_back[step]) for step in rest(final)]
    return wall([((step, outer), outer_back[step]) for step in final], wall(first, None))


def solution(mesh):
    in_specs = (P("space", "vel"), P(), P(), P(), P())
    out_specs = P("space", "vel")
    return jax.shard_map(on_device, mesh=mesh, in_specs=in_specs, out_specs=out_specs, check_vma=False)
```
